256 devices in a mesh: ctx: 32 (over y, x, core), head: 8 (over z).
Axes of the slice: x: 4, y: 4, z: 8, core: 2. Of those that a mesh axis runs over, the one named last changes fastest.
Arguments:
- tokens: bfloat16 [8192, 4096], P('ctx', 'head'), may hold values from -6 to 6
- policy_weight: bfloat16 [3, 4096, 2048], P(None, 'ctx', 'head'), may hold values from -0.09375 to 0.09375
- reference_weight: bfloat16 [3, 4096, 2048], P(None, 'ctx', 'head'), may hold values from -0.09375 to 0.09375
Outputs:
- difference: float32 [8192, 2048], P('ctx', 'head')
- input_grad: float32 [8192, 4096], P('ctx', 'head')
The draws below stay inside these ranges and needn't reach their ends.
All inputs are finite; a program needn't handle non-finite values.
Results may differ from the reference program's by a relative error of at most 0.0027.
Values may be sent and summed in bfloat16 or wider, within the bound.
A program may use at most 64 MiB of HBM per device.

```python
import math
import jax
import jax.numpy as jnp
from jax import lax

D = 4096
HD = 128
HEADS = 16
HS = 2048
TOKENS = 8192


def steps_of(key, dims, shards, low, top_value):
    gain, own = 1.0, jax.random.fold_in(key, 6)
    for axis_at, blocks in shards:
        steps = jnp.exp(jax.random.uniform(jax.random.fold_in(own, axis_at), (blocks,), jnp.float32, low / len(shards), top_value / len(shards)))
        gain = gain * jnp.repeat(steps, dims[axis_at] // blocks).reshape([-1 if axis == axis_at else 1 for axis in range(len(dims))])
    return gain


def centred(stream_key, dims, scale, limit, pieces=(), held_as=jnp.bfloat16):
    array = jax.random.normal(stream_key, dims, jnp.float32) * scale
    if len(pieces) > 0:
        array = steps_of(stream_key, dims, pieces, -0.22, 0.18) * array
    return jnp.clip(array, min=-limit, max=limit).astype(held_as)


def setup_inputs(seed: int = 0) -> dict:
    seeds = jax.random.split(jax.random.key(seed), 4)
    tokens = centred(seeds[0], (TOKENS, D), 1.0, 6.0, ((0, 32), (1, 8)))
    policy_weight = centred(seeds[1], (3, D, HS), D ** -0.5, 0.09375, ((1, 32), (2, 8)))
    reference_weight = centred(seeds[2], (3, D, HS), D ** -0.5, 0.09375, ((1, 32), (2, 8)))
    return {"tokens": tokens, "policy_weight": policy_weight, "reference_weight": reference_weight}


HIGH = lax.Precision.HIGHEST

def attend(qkv):
    block_len = math.gcd(TOKENS, 512)
    block_count = TOKENS // block_len
    query = qkv[0].reshape(block_count, block_len, HEADS, HD)
    keys = qkv[1].reshape(block_count, block_len, HEADS, HD)
    values = qkv[2].reshape(block_count, block_len, HEADS, HD)
    causal = jnp.tril(jnp.ones((block_len, block_len), jnp.float32))

    def step(state, block):
        query_block, key_block, value_block = block
        scores = jnp.einsum('thd,shd->hts', query_block, key_block, precision=HIGH) * causal
        result = jnp.einsum('hts,shd->thd', scores, value_block, precision=HIGH)
        result = result + jnp.einsum('thd,hde->the', query_block, state, precision=HIGH)
        state = state + jnp.einsum('thd,the->hde', key_block, value_block, precision=HIGH)
        return (state, result)
    start_state = jnp.zeros((HEADS, HD, HD), jnp.float32)
    _, result = lax.scan(step, start_state, (query, keys, values))
    return result.reshape(TOKENS, HEADS * HD) * (1.0 / math.sqrt(HD * TOKENS))

def reference(tokens, policy_weight, reference_weight):

    def project(weight):
        parts = [jnp.dot(tokens, weight[slot], preferred_element_type=jnp.float32) for slot in range(3)]
        return jnp.stack(parts).reshape(3, TOKENS, HEADS, HD)
    qkv_pol = project(policy_weight)
    qkv_ref = project(reference_weight)
    out_pol, pullback = jax.vjp(attend, qkv_pol)
    out_ref = attend(qkv_ref)
    difference = out_pol - out_ref
    grad_qkv, = pullback(difference)
    grad_qkv = grad_qkv.reshape(3, TOKENS, HEADS * HD).astype(jnp.bfloat16)
    input_grad = jnp.zeros((TOKENS, D), jnp.float32)
    for slot in range(3):
        input_grad = input_grad + jnp.dot(grad_qkv[slot], policy_weight[slot].T, preferred_element_type=jnp.float32)
    return (difference, input_grad)
```

```python
import functools
import math

import jax
import jax.numpy as jnp
from jax import lax
from jax.experimental import pallas as pl
from jax.experimental.pallas import tpu as pltpu
from jax.sharding import PartitionSpec as P

HD = 128
F32 = jnp.float32
BF16 = jnp.bfloat16
MESH = pl.DeviceIdType.MESH

PIECES = ((0, 1), (0, 2), (1, 1), (1, 2), (0, 0), (1, 0))
KP, VP, KR, VR, QP, QR = range(6)


def mm(a, b, ca, cb):
    return lax.dot_general(a, b, (((ca,), (cb,)), ((), ())), preferred_element_type=F32)


def split(a):
    high = a.astype(BF16)
    return high, (a - high.astype(F32)).astype(BF16)


def mm3(a, b, ca, cb):
    return mm(a[0], b[0], ca, cb) + (mm(a[0], b[1], ca, cb) + mm(a[1], b[0], ca, cb))


def kernel(
    scale, tok_ref, pol_ref, ref_ref, diff_ref, grad_ref,
    w, xs, acc, g, own_f, sib_f, chip_f, row_f, tot_f, col_f, fin_f, got_f, pre_f,
    own_b, sib_b, chip_b, row_b, tot_b, col_b, fin_b, got_b, pre_b,
    out_r, in_r, out_l, in_l,
    local_sem, p1_send, p1_recv, p2_send, p2_recv, sib_send, sib_recv,
    tok_send, tok_recv, pre_send, pre_recv, rs_send, rs_recv,
):
    ctx, z = lax.axis_index("ctx"), lax.axis_index("head")
    y, x, k = ctx // 8, lax.rem(ctx // 2, 4), lax.rem(ctx, 2)
    zs = lax.axis_size("head")

    def at(yy, xx, kk):
        return ((yy * 4 + xx) * 2 + kk, z)

    def turn(i, by):
        return lax.rem(i + by + 4, 4)

    xdev = [at(y, turn(x, d), k) for d in range(4)]
    ydev = [at(turn(y, d), x, k) for d in range(4)]
    sibling = at(y, x, 1 - k)
    zr, zl = (ctx, lax.rem(z + 1, zs)), (ctx, lax.rem(z + zs - 1, zs))

    def zb(by):
        return lax.rem(z + by + zs, zs)

    barrier = pltpu.get_barrier_semaphore()
    greeted = xdev[1:] + ydev[1:] + [sibling, zr, zl]
    for dev in greeted:
        pl.semaphore_signal(barrier, inc=1, device_id=dev, device_id_type=MESH)
    pl.semaphore_wait(barrier, len(greeted))

    sent = []

    def send(src, dst, ssem, rsem, dev):
        copy = pltpu.make_async_remote_copy(
            src_ref=src, dst_ref=dst, send_sem=ssem, recv_sem=rsem,
            device_id=dev, device_id_type=MESH,
        )
        copy.start()
        sent.append(copy)

    def arrived(dst, sem):
        pltpu.make_async_remote_copy(
            src_ref=dst, dst_ref=dst, send_sem=sem, recv_sem=sem,
            device_id=sibling, device_id_type=MESH,
        ).wait_recv()

    def source(s):
        model, slot = PIECES[s]
        return (pol_ref, ref_ref)[model].at[slot]

    def block(s, i, j):
        return w.at[s, j, i, k] if s % 2 == 0 else w.at[s, i, j, k]

    def part(s, i, j, half):
        rows = pl.ds(64 * half, 64)
        return w.at[s, j, i, k, rows] if s % 2 == 0 else w.at[s, i, j, k, rows]

    def group(s, j, kk):
        return w.at[s, j, :, kk] if s % 2 == 0 else w.at[s, :, j, kk]

    def some(s, j, half):
        few = pl.ds(2 * half, 2)
        return w.at[s, j, few, k] if s % 2 == 0 else w.at[s, few, j, k]

    def axes(s):
        return (x, y, xdev, ydev) if s % 2 == 0 else (y, x, ydev, xdev)

    def p1_start(stage):
        for s in (2 * stage, 2 * stage + 1):
            i, j, first, _ = axes(s)
            for n, d in ((0, 1), (1, 3)):
                send(source(s), block(s, i, j), p1_send.at[s, n], p1_recv.at[s, n], first[d])

    def p1_forward(stage):
        for n, d, to in ((0, -1, 1), (1, 1, 3)):
            for s in (2 * stage, 2 * stage + 1):
                i, j, first, _ = axes(s)
                arrived(block(s, turn(i, d), j), p1_recv.at[s, n])
                half = part(s, turn(i, d), j, n)
                send(half, half, p1_send.at[s, 2 + n], p1_recv.at[s, 2 + n], first[to])

    def p2_start(stage):
        for s in (2 * stage, 2 * stage + 1):
            i, j, first, second = axes(s)
            for n in range(2):
                arrived(part(s, turn(i, 2), j, n), p1_recv.at[s, 2 + n])
            mine = group(s, j, k)
            for n, d in ((0, 1), (1, 3)):
                send(mine, mine, p2_send.at[s, n], p2_recv.at[s, n], second[d])
        for s in (2 * stage, 2 * stage + 1):
            mine = group(s, axes(s)[1], k)
            send(mine, mine, sib_send.at[s, 0], sib_recv.at[s, 0], sibling)

    def p2_forward(stage):
        for n, d, to in ((0, -1, 1), (1, 1, 3)):
            for s in (2 * stage, 2 * stage + 1):
                i, j, _, second = axes(s)
                theirs = group(s, turn(j, d), k)
                arrived(theirs, p2_recv.at[s, n])
                half = some(s, turn(j, d), n)
                send(half, half, p2_send.at[s, 2 + n], p2_recv.at[s, 2 + n], second[to])
                send(theirs, theirs, sib_send.at[s, 1 + n], sib_recv.at[s, 1 + n], sibling)

    def p2_done(stage):
        for s in (2 * stage, 2 * stage + 1):
            j = axes(s)[1]
            for n in range(2):
                arrived(some(s, turn(j, 2), n), p2_recv.at[s, 2 + n])
            theirs = group(s, turn(j, 2), k)
            send(theirs, theirs, sib_send.at[s, 3], sib_recv.at[s, 3], sibling)

    def sib_done(stage):
        for s in (2 * stage, 2 * stage + 1):
            j = axes(s)[1]
            for n, d in ((0, 0), (1, -1), (2, 1), (3, 2)):
                arrived(group(s, turn(j, d), 1 - k), sib_recv.at[s, n])

    def tok(by):
        return xs.at[zb(by)]

    def tok_half(by, half):
        return xs.at[zb(by), pl.ds(128 * half, 128)]

    def tok_start():
        send(tok_ref, tok(0), tok_send.at[0, 0], tok_recv.at[0, 0], zr)
        send(tok_ref, tok(0), tok_send.at[1, 0], tok_recv.at[1, 0], zl)

    def tok_forward(step):
        for n, by, to in ((0, -step, zr), (1, step, zl)):
            arrived(tok(by), tok_recv.at[n, step - 1])
            src = tok(by) if step < 3 else tok_half(by, n)
            send(src, src, tok_send.at[n, step], tok_recv.at[n, step], to)

    def tok_done():
        for n in range(2):
            arrived(tok_half(4, n), tok_recv.at[n, 3])

    def rows_of(s, h):
        return w[s, h // 2, pl.ds(2 * lax.rem(h, 2), 2)].reshape(512, 256)

    def project(stage):
        for s in (2 * stage, 2 * stage + 1):
            acc[s] = jnp.zeros((256, 256), F32)

            @pl.loop(0, 8)
            def _(h):
                acc[s] += mm(xs[h], rows_of(s, h), 1, 0)

    def head(s, hh):
        return acc[s, :, hh * HD:(hh + 1) * HD]

    def sum_start(turn_at, own, sib):
        send(own.at[1 - k], sib, pre_send.at[turn_at, 0], pre_recv.at[turn_at, 0], sibling)

    def sum_x(turn_at, own, sib, chip, row):
        arrived(sib, pre_recv.at[turn_at, 0])
        chip[...] = own[k] + sib[...]
        for d in (2, 1, 3):
            send(chip, row.at[x], pre_send.at[turn_at, d], pre_recv.at[turn_at, d], xdev[d])

    def sum_y(turn_at, chip, row, tot, col, pre, before):
        total = chip[...]
        partial = jnp.zeros_like(total)
        for d in (1, 3, 2):
            at_x = turn(x, -d)
            arrived(row.at[at_x], pre_recv.at[turn_at, d])
            value = row[at_x]
            total += value
            partial += jnp.where(before(at_x, x), value, 0.0)
        tot[...] = total
        for d in (2, 1, 3):
            send(tot, col.at[y], pre_send.at[turn_at, 3 + d], pre_recv.at[turn_at, 3 + d], ydev[d])
        pre[...] = partial

    def sum_end(turn_at, own, sib, col, fin, got, pre, before, last):
        total = pre[...]
        for d in (1, 3, 2):
            at_y = turn(y, -d)
            arrived(col.at[at_y], pre_recv.at[turn_at, 3 + d])
            total += jnp.where(before(at_y, y), col[at_y], 0.0)
        fin[...] = total + jnp.where(k != last, own[k], 0.0)
        send(fin, got, pre_send.at[turn_at, 7], pre_recv.at[turn_at, 7], sibling)
        pre[...] = total + jnp.where(k == last, sib[...], 0.0)
        arrived(got, pre_recv.at[turn_at, 7])

    for s in range(6):
        pltpu.make_async_copy(source(s), w.at[s, y, x, k], local_sem.at[s]).start()
    pltpu.make_async_copy(tok_ref, tok(0), local_sem.at[6]).start()
    p1_start(0)
    tok_start()
    for s in range(6):
        pltpu.make_async_copy(source(s), w.at[s, y, x, k], local_sem.at[s]).wait()
    pltpu.make_async_copy(tok_ref, tok(0), local_sem.at[6]).wait()
    p1_forward(0)
    p2_start(0)
    p1_start(1)
    tok_forward(1)
    p2_forward(0)
    p1_forward(1)
    tok_forward(2)
    p2_done(0)
    p2_start(1)
    p1_start(2)
    tok_forward(3)
    p2_forward(1)
    p1_forward(2)
    p2_done(1)
    p2_start(2)
    tok_done()
    sib_done(0)
    project(0)
    for hh in range(2):
        own_f[hh, 0] = mm3(split(head(KP, hh)), split(head(VP, hh)), 0, 0)
    sib_done(1)
    project(1)
    for hh in range(2):
        own_f[hh, 1] = mm3(split(head(KR, hh)), split(head(VR, hh)), 0, 0)
    earlier = lambda a, b: a < b
    later = lambda a, b: a > b
    sum_start(0, own_f, sib_f)
    p2_forward(2)
    sum_x(0, own_f, sib_f, chip_f, row_f)
    p2_done(2)
    sum_y(0, chip_f, row_f, tot_f, col_f, pre_f, earlier)
    sib_done(2)
    project(2)
    sum_end(0, own_f, sib_f, col_f, fin_f, got_f, pre_f, earlier, 1)

    rows = lax.broadcasted_iota(jnp.int32, (256, 256), 0)
    columns = lax.broadcasted_iota(jnp.int32, (256, 256), 1)
    causal = rows >= columns

    def prefix(model, hh):
        return jnp.where(k == hh, pre_f[model], got_f[model])

    for hh in range(2):
        cols = slice(hh * HD, (hh + 1) * HD)
        outs = []
        for model, (qs, ks, vs) in enumerate(((QP, KP, VP), (QR, KR, VR))):
            q, kk, v = (split(head(s, hh)) for s in (qs, ks, vs))
            scores = split(jnp.where(causal, mm3(q, kk, 1, 1), 0.0))
            outs.append(
                scale * (mm3(scores, v, 1, 0) + mm3(q, split(prefix(model, hh)), 1, 0))
            )
        diff = outs[0] - outs[1]
        diff_ref[:, cols] = diff
        own_b[hh] = mm3(split(head(QP, hh)), split(diff), 0, 0)
    sum_start(1, own_b, sib_b)
    sum_x(1, own_b, sib_b, chip_b, row_b)

    for hh in range(2):
        cols = slice(hh * HD, (hh + 1) * HD)
        q, kk, v = (split(head(s, hh)) for s in (QP, KP, VP))
        diff = split(diff_ref[:, cols])
        weighted = split(jnp.where(causal, mm3(diff, v, 1, 1), 0.0))
        scores = split(jnp.where(causal, mm3(q, kk, 1, 1), 0.0))
        dq = mm3(weighted, kk, 1, 0) + mm3(diff, split(prefix(0, hh)), 1, 1)
        g[0, :, cols] = (scale * dq).astype(BF16)
        acc[KR, :, cols] = mm3(weighted, q, 0, 0)
        acc[VR, :, cols] = mm3(scores, diff, 0, 0)
        if hh == 0:
            sum_y(1, chip_b, row_b, tot_b, col_b, pre_b, later)
    sum_end(1, own_b, sib_b, col_b, fin_b, got_b, pre_b, later, 0)
    for hh in range(2):
        cols = slice(hh * HD, (hh + 1) * HD)
        kk, v = (split(head(s, hh)) for s in (KP, VP))
        suffix = split(jnp.where(k == hh, pre_b[...], got_b[...]))
        g[1, :, cols] = (scale * (acc[KR, :, cols] + mm3(v, suffix, 1, 1))).astype(BF16)
        g[2, :, cols] = (scale * (acc[VR, :, cols] + mm3(kk, suffix, 1, 0))).astype(BF16)

    def term(by, half):
        h, few = zb(by), slice(128 * half, 128 * half + 128)
        return (
            mm(g[0, few], rows_of(QP, h), 1, 1)
            + mm(g[1, few], rows_of(KP, h), 1, 1)
            + mm(g[2, few], rows_of(VP, h), 1, 1)
        )

    def hop(n, sign, out, inn, to, step, half):
        value = term(sign * (5 - step), half)
        fresh = step == 1 or (step == 2 and half != n)
        if not fresh:
            arrived(inn.at[step - 2, half], rs_recv.at[n, step - 2, half])
            value = value + inn[step - 2, half].astype(F32)
        out[step - 1, half] = value.astype(BF16)
        send(
            out.at[step - 1, half], inn.at[step - 1, half],
            rs_send.at[n, step - 1, half], rs_recv.at[n, step - 1, half], to,
        )

    ways = ((0, 1, out_r, in_r, zr), (1, -1, out_l, in_l, zl))
    for step in range(1, 5):
        for turn_at in range(2):
            for n, sign, out, inn, to in ways:
                half = (1 - n) if turn_at == 0 else n
                if step == 1 and half != n:
                    continue
                hop(n, sign, out, inn, to, step, half)
    for half in range(2):
        few = slice(128 * half, 128 * half + 128)
        grad_ref[few] = term(0, half)
    for turn_at in range(2):
        for n, _, _, inn, _ in ways:
            half = (1 - n) if turn_at == 0 else n
            few = slice(128 * half, 128 * half + 128)
            arrived(inn.at[3, half], rs_recv.at[n, 3, half])
            grad_ref[few] += inn[3, half].astype(F32)
    for copy in sent:
        copy.wait_send()


def per_device(tokens, policy_weight, reference_weight):
    seq = tokens.shape[0] * lax.axis_size("ctx")
    scale = 1.0 / math.sqrt(HD * seq)
    state = lambda *lead: pltpu.VMEM((*lead, HD, HD), F32)
    half = pltpu.VMEM((4, 2, 128, 512), BF16)
    dma = pltpu.SemaphoreType.DMA
    return pl.pallas_call(
        functools.partial(kernel, scale),
        out_shape=(
            jax.ShapeDtypeStruct((256, 256), F32),
            jax.ShapeDtypeStruct((256, 512), F32),
        ),
        in_specs=[pl.BlockSpec(memory_space=pl.ANY)] * 3,
        out_specs=[pl.BlockSpec(memory_space=pltpu.VMEM)] * 2,
        scratch_shapes=[
            pltpu.VMEM((6, 4, 4, 2, 128, 256), BF16),
            pltpu.VMEM((8, 256, 512), BF16),
            pltpu.VMEM((6, 256, 256), F32),
            pltpu.VMEM((3, 256, 256), BF16),
            state(2, 2), state(2), state(2), state(4, 2), state(2), state(4, 2),
            state(2), state(2), state(2),
            state(2), state(), state(), state(4), state(), state(4), state(), state(), state(),
            half, half, half, half,
            dma((7,)), dma((6, 4)), dma((6, 4)), dma((6, 4)), dma((6, 4)),
            dma((6, 4)), dma((6, 4)), dma((2, 4)), dma((2, 4)), dma((2, 8)), dma((2, 8)),
            dma((2, 4, 2)), dma((2, 4, 2)),
        ],
        compiler_params=pltpu.CompilerParams(
            collective_id=0, has_side_effects=True, vmem_limit_bytes=58 * 2**20
        ),
    )(tokens, policy_weight, reference_weight)


def solution(mesh):
    in_specs = (P("ctx", "head"), P(None, "ctx", "head"), P(None, "ctx", "head"))
    out_specs = (P("ctx", "head"), P("ctx", "head"))
    return jax.shard_map(
        per_device, mesh=mesh, in_specs=in_specs, out_specs=out_specs, check_vma=False
    )
```

```python
import functools
import math

import jax
import jax.numpy as jnp
from jax import lax
from jax.experimental import pallas as pl
from jax.experimental.pallas import tpu as pltpu
from jax.sharding import PartitionSpec as P

HD = 128
F32 = jnp.float32
BF16 = jnp.bfloat16
MESH = pl.DeviceIdType.MESH

PIECES = ((0, 1), (0, 2), (1, 1), (1, 2), (0, 0), (1, 0))
KP, VP, KR, VR, QP, QR = range(6)


def mm(a, b, ca, cb):
    return lax.dot_general(a, b, (((ca,), (cb,)), ((), ())), preferred_element_type=F32)


def split(a):
    high = a.astype(BF16)
    return high, (a - high.astype(F32)).astype(BF16)


def mm3(a, b, ca, cb):
    return mm(a[0], b[0], ca, cb) + (mm(a[0], b[1], ca, cb) + mm(a[1], b[0], ca, cb))


def kernel(
    scale, tok_ref, pol_ref, ref_ref, diff_ref, grad_ref,
    w, xs, acc, att, sc, g, own_f, sib_f, chip_f, got1_f, msg_f, got2_f, fin_f, got_f, pre_f,
    own_b, sib_b, chip_b, got1_b, msg_b, got2_b, fin_b, got_b, pre_b,
    out_r, in_r, out_l, in_l,
    local_sem, p1_send, p1_recv, p2_send, p2_recv, sib_send, sib_recv,
    tok_send, tok_recv, pre_send, pre_recv, rs_send, rs_recv,
):
    ctx, z = lax.axis_index("ctx"), lax.axis_index("head")
    y, x, k = ctx // 8, lax.rem(ctx // 2, 4), lax.rem(ctx, 2)
    zs = lax.axis_size("head")

    def at(yy, xx, kk):
        return ((yy * 4 + xx) * 2 + kk, z)

    def turn(i, by):
        return lax.rem(i + by + 4, 4)

    xdev = [at(y, turn(x, d), k) for d in range(4)]
    ydev = [at(turn(y, d), x, k) for d in range(4)]
    sibling = at(y, x, 1 - k)
    zr, zl = (ctx, lax.rem(z + 1, zs)), (ctx, lax.rem(z + zs - 1, zs))

    def zb(by):
        return lax.rem(z + by + zs, zs)

    barrier = pltpu.get_barrier_semaphore()
    greeted = xdev[1:] + ydev[1:] + [sibling, zr, zl]
    for dev in greeted:
        pl.semaphore_signal(barrier, inc=1, device_id=dev, device_id_type=MESH)
    pl.semaphore_wait(barrier, len(greeted))

    sent = []

    def send(src, dst, ssem, rsem, dev):
        copy = pltpu.make_async_remote_copy(
            src_ref=src, dst_ref=dst, send_sem=ssem, recv_sem=rsem,
            device_id=dev, device_id_type=MESH,
        )
        copy.start()
        sent.append(copy)

    def arrived(dst, sem):
        pltpu.make_async_remote_copy(
            src_ref=dst, dst_ref=dst, send_sem=sem, recv_sem=sem,
            device_id=sibling, device_id_type=MESH,
        ).wait_recv()

    def source(s):
        model, slot = PIECES[s]
        return (pol_ref, ref_ref)[model].at[slot]

    def block(s, i, j):
        return w.at[s, j, i, k] if s % 2 == 0 else w.at[s, i, j, k]

    def part(s, i, j, half):
        rows = pl.ds(64 * half, 64)
        return w.at[s, j, i, k, rows] if s % 2 == 0 else w.at[s, i, j, k, rows]

    def group(s, j, kk):
        return w.at[s, j, :, kk] if s % 2 == 0 else w.at[s, :, j, kk]

    def some(s, j, half, kk):
        few = pl.ds(2 * half, 2)
        return w.at[s, j, few, kk] if s % 2 == 0 else w.at[s, few, j, kk]

    def axes(s):
        return (x, y, xdev, ydev) if s % 2 == 0 else (y, x, ydev, xdev)

    def pair(stage):
        return (2 * stage, 2 * stage + 1)

    def p1_start(stage):
        for s in pair(stage):
            i, j, first, _ = axes(s)
            for n, d in ((0, 1), (1, 3)):
                send(source(s), block(s, i, j), p1_send.at[s, n], p1_recv.at[s, n], first[d])

    def p1_forward(stage):
        for n, d, to in ((0, -1, 1), (1, 1, 3)):
            for s in pair(stage):
                i, j, first, _ = axes(s)
                arrived(block(s, turn(i, d), j), p1_recv.at[s, n])
                half = part(s, turn(i, d), j, n)
                send(half, half, p1_send.at[s, 2 + n], p1_recv.at[s, 2 + n], first[to])

    def p1_done(stage):
        for s in pair(stage):
            i, j, _, _ = axes(s)
            for n in range(2):
                arrived(part(s, turn(i, 2), j, n), p1_recv.at[s, 2 + n])

    def p2_start(stage):
        for later_half in range(2):
            for s in pair(stage):
                _, j, _, second = axes(s)
                for n, d in ((0, 1), (1, 3)):
                    mine = some(s, j, n ^ later_half, k)
                    at_n = 2 * n + later_half
                    send(mine, mine, p2_send.at[s, at_n], p2_recv.at[s, at_n], second[d])

    def sib_start(stage):
        for s in pair(stage):
            mine = group(s, axes(s)[1], k)
            send(mine, mine, sib_send.at[s, 0], sib_recv.at[s, 0], sibling)

    def p2_forward(stage):
        for n, d, to in ((0, -1, 1), (1, 1, 3)):
            for s in pair(stage):
                _, j, _, second = axes(s)
                half = some(s, turn(j, d), n, k)
                arrived(half, p2_recv.at[s, 2 * n])
                send(half, half, p2_send.at[s, 4 + n], p2_recv.at[s, 4 + n], second[to])

    def p2_sides(stage):
        for n, d in ((0, -1), (1, 1)):
            for s in pair(stage):
                j = axes(s)[1]
                arrived(some(s, turn(j, d), 1 - n, k), p2_recv.at[s, 2 * n + 1])
                theirs = group(s, turn(j, d), k)
                send(theirs, theirs, sib_send.at[s, 1 + n], sib_recv.at[s, 1 + n], sibling)

    def p2_done(stage):
        for n in range(2):
            for s in pair(stage):
                half = some(s, turn(axes(s)[1], 2), n, k)
                arrived(half, p2_recv.at[s, 4 + n])
                send(half, half, sib_send.at[s, 3 + n], sib_recv.at[s, 3 + n], sibling)

    def sib_sides(stage):
        for s in pair(stage):
            j = axes(s)[1]
            for n, d in ((0, 0), (1, -1), (2, 1)):
                arrived(group(s, turn(j, d), 1 - k), sib_recv.at[s, n])

    def sib_done(stage):
        for s in pair(stage):
            for n in range(2):
                arrived(some(s, turn(axes(s)[1], 2), n, 1 - k), sib_recv.at[s, 3 + n])

    def tok(by, c):
        return xs.at[2 * zb(by) + c]

    def tok_start():
        for c in range(2):
            for n, to in ((0, zr), (1, zl)):
                cc = c ^ n
                src = tok_ref.at[:, pl.ds(256 * cc, 256)]
                send(src, tok(0, cc), tok_send.at[n, 0, cc], tok_recv.at[n, 0, cc], to)

    def tok_forward(step):
        for c in range(2):
            for n, by, to in ((0, -step, zr), (1, step, zl)):
                cc = c ^ n
                arrived(tok(by, cc), tok_recv.at[n, step - 1, cc])
                if step < 3 or c == 0:
                    send(
                        tok(by, cc), tok(by, cc),
                        tok_send.at[n, step, cc], tok_recv.at[n, step, cc], to,
                    )

    def tok_done():
        for n in range(2):
            arrived(tok(4, n), tok_recv.at[n, 3, n])

    def chunk(s, f):
        return w[s, f // 4, lax.rem(f, 4)].reshape(256, 256)

    def add_chunks(s, chunks, first):
        total = acc[s] if not first else None
        for f in chunks:
            value = mm(xs[f], chunk(s, f), 1, 0)
            total = value if total is None else total + value
        acc[s] = total

    def project_tokens(stage, places, first=False):
        for s in pair(stage):
            add_chunks(s, [2 * zb(by) + c for by in places for c in range(2)], first)

    def project_group(stage, d, first=False):
        for s in pair(stage):
            j = turn(axes(s)[1], d)
            add_chunks(s, [4 * j + i if s % 2 == 0 else 4 * i + j for i in range(4)], first)

    def head(s, hh):
        return acc[s, :, hh * HD:(hh + 1) * HD]

    up, low = pl.ds(0, 64), pl.ds(64, 64)

    def rows_in(ref, lead, few):
        inner = len(ref.shape) - len(lead) - 2
        return ref.at[(*lead, *[slice(None)] * inner, few)]

    def sum_start(t, own, sib):
        send(own.at[1 - k], sib, pre_send.at[t, 0], pre_recv.at[t, 0], sibling)

    def sum_one(t, own, sib, chip, got1):
        arrived(sib, pre_recv.at[t, 0])
        chip[...] = own[k] + sib[...]
        for d in (2, 1, 3):
            for q, devs, i, few in ((0, xdev, x, up), (1, ydev, y, low)):
                at_n = 3 * q + d
                send(
                    rows_in(chip, (), few), got1.at[q, i],
                    pre_send.at[t, at_n], pre_recv.at[t, at_n], devs[d],
                )

    def sum_two(t, chip, got1, msg, got2, pre, before):
        total = rows_in(chip, (), up)[...]
        partial = jnp.zeros_like(total)
        ahead = jnp.zeros_like(total)
        for d in (1, 3, 2):
            at_x, at_y = turn(x, -d), turn(y, -d)
            arrived(got1.at[0, at_x], pre_recv.at[t, d])
            value = got1[0, at_x]
            total += value
            partial += jnp.where(before(at_x, x), value, 0.0)
            arrived(got1.at[1, at_y], pre_recv.at[t, 3 + d])
            ahead += jnp.where(before(at_y, y), got1[1, at_y], 0.0)
        msg[0] = total
        msg[1] = ahead
        msg[2] = ahead + rows_in(chip, (), low)[...]
        rows_in(pre, (), up)[...] = partial
        rows_in(pre, (), low)[...] = ahead
        for d in (2, 1, 3):
            send(
                msg.at[0], got2.at[0, y],
                pre_send.at[t, 6 + d], pre_recv.at[t, 6 + d], ydev[d],
            )
            which = jnp.where(before(x, turn(x, d)), 2, 1)
            send(
                msg.at[which], got2.at[1, x],
                pre_send.at[t, 9 + d], pre_recv.at[t, 9 + d], xdev[d],
            )

    def sum_three(t, own, sib, got2, fin, got, pre, before, last):
        upper, lower = rows_in(pre, (), up)[...], rows_in(pre, (), low)[...]
        for d in (1, 3, 2):
            at_x, at_y = turn(x, -d), turn(y, -d)
            arrived(got2.at[0, at_y], pre_recv.at[t, 6 + d])
            upper += jnp.where(before(at_y, y), got2[0, at_y], 0.0)
            arrived(got2.at[1, at_x], pre_recv.at[t, 9 + d])
            lower += got2[1, at_x]
        rows_in(pre, (), up)[...] = upper
        rows_in(pre, (), low)[...] = lower
        total = pre[...]
        fin[...] = total + jnp.where(k != last, own[k], 0.0)
        send(fin, got, pre_send.at[t, 13], pre_recv.at[t, 13], sibling)
        pre[...] = total + jnp.where(k == last, sib[...], 0.0)

    def sum_four(t, got):
        arrived(got, pre_recv.at[t, 13])

    earlier = lambda a, b: a < b
    later = lambda a, b: a > b

    def copies():
        yield from (
            pltpu.make_async_copy(source(s), w.at[s, y, x, k], local_sem.at[s])
            for s in range(6)
        )
        yield from (
            pltpu.make_async_copy(
                tok_ref.at[:, pl.ds(256 * c, 256)], tok(0, c), local_sem.at[6 + c]
            )
            for c in range(2)
        )

    for stage in range(3):
        p1_start(stage)
    tok_start()
    for copy in copies():
        copy.start()
    for copy in copies():
        copy.wait()
    for stage in range(3):
        p1_forward(stage)
    p1_done(0)
    p2_start(0)
    sib_start(0)
    p1_done(1)
    p1_done(2)
    tok_forward(1)
    p2_forward(0)
    p2_start(1)
    sib_start(1)
    tok_forward(2)
    p2_sides(0)
    p2_done(0)
    tok_forward(3)
    sib_sides(0)
    sib_done(0)
    project_tokens(0, (0, -1), True)
    p2_forward(1)
    p2_start(2)
    sib_start(2)
    project_tokens(0, (1, -2))
    project_tokens(0, (2, -3))
    p2_sides(1)
    tok_done()
    project_tokens(0, (3, 4))
    for hh in range(2):
        own_f[hh, 0] = mm3(split(head(KP, hh)), split(head(VP, hh)), 0, 0)
    sib_sides(1)
    project_group(1, 0, True)
    p2_done(1)
    project_group(1, -1)
    project_group(1, 1)
    sib_done(1)
    project_group(1, 2)
    for hh in range(2):
        own_f[hh, 1] = mm3(split(head(KR, hh)), split(head(VR, hh)), 0, 0)
    sum_start(0, own_f, sib_f)
    p2_forward(2)
    sum_one(0, own_f, sib_f, chip_f, got1_f)
    p2_sides(2)
    sib_sides(2)
    project_group(2, 0, True)
    project_group(2, -1)
    sum_two(0, chip_f, got1_f, msg_f, got2_f, pre_f, earlier)
    project_group(2, 1)
    p2_done(2)
    sib_done(2)
    project_group(2, 2)

    rows = lax.broadcasted_iota(jnp.int32, (256, 256), 0)
    columns = lax.broadcasted_iota(jnp.int32, (256, 256), 1)
    causal = rows >= columns

    def prefix(model, hh):
        return jnp.where(k == hh, pre_f[model], got_f[model])

    PAIRS = ((QP, KP, VP), (QR, KR, VR))
    for hh in range(2):
        cols = slice(hh * HD, (hh + 1) * HD)
        for model, (qs, ks, vs) in enumerate(PAIRS):
            q, kk, v = (split(head(s, hh)) for s in (qs, ks, vs))
            scores = split(jnp.where(causal, mm3(q, kk, 1, 1), 0.0))
            att[model, :, cols] = mm3(scores, v, 1, 0)
            if model == 0:
                sc[hh, 0], sc[hh, 1] = scores
    sum_three(0, own_f, sib_f, got2_f, fin_f, got_f, pre_f, earlier, 1)
    sum_four(0, got_f)
    for hh in range(2):
        cols = slice(hh * HD, (hh + 1) * HD)
        outs = [
            scale * (att[m, :, cols] + mm3(split(head(qs, hh)), split(prefix(m, hh)), 1, 0))
            for m, qs in enumerate((QP, QR))
        ]
        diff = outs[0] - outs[1]
        diff_ref[:, cols] = diff
        own_b[hh] = mm3(split(head(QP, hh)), split(diff), 0, 0)
    sum_start(1, own_b, sib_b)
    sum_one(1, own_b, sib_b, chip_b, got1_b)

    for hh in range(2):
        cols = slice(hh * HD, (hh + 1) * HD)
        q, kk, v = (split(head(s, hh)) for s in (QP, KP, VP))
        diff = split(diff_ref[:, cols])
        weighted = split(jnp.where(causal, mm3(diff, v, 1, 1), 0.0))
        dq = mm3(weighted, kk, 1, 0) + mm3(diff, split(prefix(0, hh)), 1, 1)
        g[0, :, cols] = (scale * dq).astype(BF16)
        att[0, :, cols] = mm3(weighted, q, 0, 0)
        att[1, :, cols] = mm3((sc[hh, 0], sc[hh, 1]), diff, 0, 0)
        if hh == 0:
            sum_two(1, chip_b, got1_b, msg_b, got2_b, pre_b, later)
    sum_three(1, own_b, sib_b, got2_b, fin_b, got_b, pre_b, later, 0)
    sum_four(1, got_b)
    for hh in range(2):
        cols = slice(hh * HD, (hh + 1) * HD)
        kk, v = (split(head(s, hh)) for s in (KP, VP))
        suffix = split(jnp.where(k == hh, pre_b[...], got_b[...]))
        g[1, :, cols] = (scale * (att[0, :, cols] + mm3(v, suffix, 1, 1))).astype(BF16)
        g[2, :, cols] = (scale * (att[1, :, cols] + mm3(kk, suffix, 1, 0))).astype(BF16)

    def rows_of(s, h):
        return w[s, h // 2, pl.ds(2 * lax.rem(h, 2), 2)].reshape(512, 256)

    def term(by, half):
        h, few = zb(by), slice(128 * half, 128 * half + 128)
        return (
            mm(g[0, few], rows_of(QP, h), 1, 1)
            + mm(g[1, few], rows_of(KP, h), 1, 1)
            + mm(g[2, few], rows_of(VP, h), 1, 1)
        )

    def hop(n, sign, out, inn, to, step, half):
        value = term(sign * (5 - step), half)
        fresh = step == 1 or (step == 2 and half != n)
        if not fresh:
            arrived(inn.at[step - 2, half], rs_recv.at[n, step - 2, half])
            value = value + inn[step - 2, half].astype(F32)
        out[step - 1, half] = value.astype(BF16)
        send(
            out.at[step - 1, half], inn.at[step - 1, half],
            rs_send.at[n, step - 1, half], rs_recv.at[n, step - 1, half], to,
        )

    ways = ((0, 1, out_r, in_r, zr), (1, -1, out_l, in_l, zl))
    for step in range(1, 5):
        for turn_at in range(2):
            for n, sign, out, inn, to in ways:
                half = (1 - n) if turn_at == 0 else n
                if step == 1 and half != n:
                    continue
                hop(n, sign, out, inn, to, step, half)
    for half in range(2):
        few = slice(128 * half, 128 * half + 128)
        grad_ref[few] = term(0, half)
    for turn_at in range(2):
        for n, _, _, inn, _ in ways:
            half = (1 - n) if turn_at == 0 else n
            few = slice(128 * half, 128 * half + 128)
            arrived(inn.at[3, half], rs_recv.at[n, 3, half])
            grad_ref[few] += inn[3, half].astype(F32)
    for copy in sent:
        copy.wait_send()


def per_device(tokens, policy_weight, reference_weight):
    seq = tokens.shape[0] * lax.axis_size("ctx")
    scale = 1.0 / math.sqrt(HD * seq)

    def sums(*models):
        whole = pltpu.VMEM((*models, HD, HD), F32)
        some = lambda *lead: pltpu.VMEM((*lead, *models, HD // 2, HD), F32)
        own = pltpu.VMEM((2, *models, HD, HD), F32)
        return own, whole, whole, some(2, 4), some(3), some(2, 4), whole, whole, whole

    half = pltpu.VMEM((4, 2, 128, 512), BF16)
    dma = pltpu.SemaphoreType.DMA
    return pl.pallas_call(
        functools.partial(kernel, scale),
        out_shape=(
            pltpu.VMEM((256, 256), F32),
            pltpu.VMEM((256, 512), F32),
        ),
        in_specs=[pl.BlockSpec(memory_space=pl.ANY)] * 3,
        out_specs=[pl.BlockSpec(memory_space=pltpu.VMEM)] * 2,
        scratch_shapes=[
            pltpu.VMEM((6, 4, 4, 2, 128, 256), BF16),
            pltpu.VMEM((16, 256, 256), BF16),
            pltpu.VMEM((6, 256, 256), F32),
            pltpu.VMEM((2, 256, 256), F32),
            pltpu.VMEM((2, 2, 256, 256), BF16),
            pltpu.VMEM((3, 256, 256), BF16),
            *sums(2),
            *sums(),
            half, half, half, half,
            dma((8,)), dma((6, 4)), dma((6, 4)), dma((6, 6)), dma((6, 6)), dma((6, 5)),
            dma((6, 5)), dma((2, 4, 2)), dma((2, 4, 2)), dma((2, 14)), dma((2, 14)),
            dma((2, 4, 2)), dma((2, 4, 2)),
        ],
        compiler_params=pltpu.CompilerParams(
            collective_id=0, has_side_effects=True, vmem_limit_bytes=58 * 2**20
        ),
    )(tokens, policy_weight, reference_weight)


def solution(mesh):
    in_specs = (P("ctx", "head"), P(None, "ctx", "head"), P(None, "ctx", "head"))
    out_specs = (P("ctx", "head"), P("ctx", "head"))
    return jax.shard_map(
        per_device, mesh=mesh, in_specs=in_specs, out_specs=out_specs, check_vma=False
    )
```

```python
import functools
import math

import jax
import jax.numpy as jnp
from jax import lax
from jax.experimental import pallas as pl
from jax.experimental.pallas import tpu as pltpu
from jax.sharding import PartitionSpec as P

HD = 128
F32 = jnp.float32
BF16 = jnp.bfloat16
MESH = pl.DeviceIdType.MESH

PIECES = ((0, 1), (0, 2), (1, 1), (1, 2), (0, 0), (1, 0))
KP, VP, KR, VR, QP, QR = range(6)


def mm(a, b, ca, cb):
    return lax.dot_general(a, b, (((ca,), (cb,)), ((), ())), preferred_element_type=F32)


def split(a):
    high = a.astype(BF16)
    return high, (a - high.astype(F32)).astype(BF16)


def mm3(a, b, ca, cb):
    return mm(a[0], b[0], ca, cb) + (mm(a[0], b[1], ca, cb) + mm(a[1], b[0], ca, cb))


def kernel(
    scale, tok_ref, pol_ref, ref_ref, diff_ref, grad_ref,
    w, w2, xs, acc, att, sc, ed, dgot, g, gx, sums,
    out_r, in_r, out_l, in_l,
    local_sem, give_send, give_recv, p1_send, p1_recv, p2_send, p2_recv, sib_send, sib_recv,
    tok_send, tok_recv, pre_send, pre_recv, rs_send, rs_recv,
):
    ctx, z = lax.axis_index("ctx"), lax.axis_index("head")
    y, x, k = ctx // 8, lax.rem(ctx // 2, 4), lax.rem(ctx, 2)
    zs = lax.axis_size("head")

    def at(yy, xx, kk):
        return ((yy * 4 + xx) * 2 + kk, z)

    def turn(i, by):
        return lax.rem(i + by + 4, 4)

    xdev = [at(y, turn(x, d), k) for d in range(4)]
    ydev = [at(turn(y, d), x, k) for d in range(4)]
    sibling = at(y, x, 1 - k)
    zr, zl = (ctx, lax.rem(z + 1, zs)), (ctx, lax.rem(z + zs - 1, zs))

    def zb(by):
        return lax.rem(z + by + zs, zs)

    barrier = pltpu.get_barrier_semaphore()
    greeted = xdev[1:] + ydev[1:] + [sibling, zr, zl]
    for dev in greeted:
        pl.semaphore_signal(barrier, inc=1, device_id=dev, device_id_type=MESH)
    pl.semaphore_wait(barrier, len(greeted))

    sent = []

    def send(src, dst, ssem, rsem, dev):
        copy = pltpu.make_async_remote_copy(
            src_ref=src, dst_ref=dst, send_sem=ssem, recv_sem=rsem,
            device_id=dev, device_id_type=MESH,
        )
        copy.start()
        sent.append(copy)

    def arrived(dst, sem):
        pltpu.make_async_remote_copy(
            src_ref=dst, dst_ref=dst, send_sem=sem, recv_sem=sem,
            device_id=sibling, device_id_type=MESH,
        ).wait_recv()

    def lanes(kk):
        return pl.ds(pl.multiple_of(HD * kk, HD), HD)

    def half_rows(p):
        return pl.ds(pl.multiple_of(128 * p, 128), 128)

    def core_rows(kk):
        return pl.ds(pl.multiple_of(256 * kk, 256), 256)

    def source(s, kk):
        model, slot = PIECES[s]
        return (pol_ref, ref_ref)[model].at[slot, :, lanes(kk)]

    def block(s, i, j):
        return w.at[s, j, i] if s % 2 == 0 else w.at[s, i, j]

    def part(s, i, j, p):
        rows = half_rows(p)
        return w.at[s, j, i, rows] if s % 2 == 0 else w.at[s, i, j, rows]

    def some(s, j, half):
        few = pl.ds(2 * half, 2)
        return w.at[s, j, few] if s % 2 == 0 else w.at[s, few, j]

    def axes(s):
        return (x, y, xdev, ydev) if s % 2 == 0 else (y, x, ydev, xdev)

    def pair(stage):
        return (2 * stage, 2 * stage + 1)

    def give(stage):
        for s in pair(stage):
            send(
                source(s, 1 - k), w.at[s, y, x, half_rows(k)],
                give_send.at[s], give_recv.at[s], sibling,
            )

    def p1_start(stage):
        for s in pair(stage):
            i, j, first, _ = axes(s)
            for n, d in ((0, 1), (1, 3)):
                at_n = 2 * n + k
                send(
                    source(s, k), part(s, i, j, k),
                    p1_send.at[s, at_n], p1_recv.at[s, at_n], first[d],
                )

    def p1_given(stage):
        for s in pair(stage):
            i, j, first, _ = axes(s)
            given = part(s, i, j, 1 - k)
            arrived(given, give_recv.at[s])
            for n, d in ((0, 1), (1, 3)):
                at_n = 2 * n + 1 - k
                send(given, given, p1_send.at[s, at_n], p1_recv.at[s, at_n], first[d])

    def p1_forward(stage):
        for n, d, to in ((0, -1, 1), (1, 1, 3)):
            for s in pair(stage):
                i, j, first, _ = axes(s)
                half = part(s, turn(i, d), j, n)
                arrived(half, p1_recv.at[s, 3 * n])
                send(half, half, p1_send.at[s, 4 + n], p1_recv.at[s, 4 + n], first[to])

    def p1_done(stage):
        for s in pair(stage):
            i, j, _, _ = axes(s)
            for n, d in ((0, -1), (1, 1)):
                arrived(part(s, turn(i, d), j, 1 - n), p1_recv.at[s, 1 + n])
            for n in range(2):
                arrived(part(s, turn(i, 2), j, n), p1_recv.at[s, 4 + n])

    def p2_start(stage, second_half):
        for s in pair(stage):
            _, j, _, second = axes(s)
            for n, d in ((0, 1), (1, 3)):
                mine = some(s, j, n ^ second_half)
                at_n = 2 * n + second_half
                send(mine, mine, p2_send.at[s, at_n], p2_recv.at[s, at_n], second[d])

    def p2_forward(stage):
        for n, d, to in ((0, -1, 1), (1, 1, 3)):
            for s in pair(stage):
                _, j, _, second = axes(s)
                half = some(s, turn(j, d), n)
                arrived(half, p2_recv.at[s, 2 * n])
                send(half, half, p2_send.at[s, 4 + n], p2_recv.at[s, 4 + n], second[to])

    def p2_sides(stage):
        for n, d in ((0, -1), (1, 1)):
            for s in pair(stage):
                arrived(some(s, turn(axes(s)[1], d), 1 - n), p2_recv.at[s, 2 * n + 1])

    def p2_done(stage):
        for n in range(2):
            for s in pair(stage):
                arrived(some(s, turn(axes(s)[1], 2), n), p2_recv.at[s, 4 + n])

    def share(s, at_n):
        send(w.at[s], w2.at[at_n], sib_send.at[at_n], sib_recv.at[at_n], sibling)

    def tok(by, c):
        return xs.at[2 * zb(by) + c, core_rows(k)]

    def tok_both(by, kk):
        return xs.at[pl.ds(2 * zb(by), 2), core_rows(kk)]

    def tok_share(by, at_n):
        mine = tok_both(by, k)
        send(mine, mine, sib_send.at[at_n], sib_recv.at[at_n], sibling)

    def tok_shared(by, at_n):
        arrived(tok_both(by, 1 - k), sib_recv.at[at_n])

    def tok_start():
        for c in range(2):
            for n, to in ((0, zr), (1, zl)):
                cc = c ^ n
                src = tok_ref.at[:, pl.ds(256 * cc, 256)]
                send(src, tok(0, cc), tok_send.at[n, 0, cc], tok_recv.at[n, 0, cc], to)

    def tok_forward(step):
        for c in range(2):
            for n, by, to in ((0, -step, zr), (1, step, zl)):
                cc = c ^ n
                arrived(tok(by, cc), tok_recv.at[n, step - 1, cc])
                if step < 3 or c == 0:
                    send(
                        tok(by, cc), tok(by, cc),
                        tok_send.at[n, step, cc], tok_recv.at[n, step, cc], to,
                    )
        tok_share(-step, 3 + 2 * step)
        tok_share(step, 4 + 2 * step)

    def tok_done():
        for n in range(2):
            arrived(tok(4, n), tok_recv.at[n, 3, n])
        tok_share(4, 4)

    def both(ref, first, second, f):
        at_f = (f // 4, lax.rem(f, 4))
        return jnp.concatenate([ref[first, *at_f], ref[second, *at_f]], 1)

    def add_chunks(stage, chunks, first):
        total = acc[stage] if not first else None
        for f in chunks:
            value = mm(xs[f], both(w, *pair(stage), f), 1, 0)
            total = value if total is None else total + value
        acc[stage] = total

    def project_tokens(stage, places, first=False):
        add_chunks(stage, [2 * zb(by) + c for by in places for c in range(2)], first)

    def project_rows(stage, yy, first=False):
        add_chunks(stage, [4 * yy + i for i in range(4)], first)

    def project_apart(stage, d, first=False):
        for s in pair(stage):
            j = turn(axes(s)[1], d)
            cols = slice(HD * (s % 2), HD * (s % 2) + HD)
            total = acc[stage, :, cols] if not first else None
            for i in range(4):
                at_f = (j, i) if s % 2 == 0 else (i, j)
                value = mm(xs[4 * at_f[0] + at_f[1]], w[s, *at_f], 1, 0)
                total = value if total is None else total + value
            acc[stage, :, cols] = total

    def piece(s):
        return acc[s // 2, :, (s % 2) * HD:(s % 2 + 1) * HD]

    up, low = pl.ds(0, 64), pl.ds(64, 64)

    def sum_one(t):
        chip, got1 = sums[t][:2]
        for d in (2, 1, 3):
            for q, devs, i, few in ((0, xdev, x, up), (1, ydev, y, low)):
                at_n = 3 * q + d - 1
                send(
                    chip.at[few], got1.at[q, i],
                    pre_send.at[t, at_n], pre_recv.at[t, at_n], devs[d],
                )

    def sum_two(t, before):
        chip, got1, msg, got2, pre = sums[t]
        total = chip[:64]
        partial = jnp.zeros_like(total)
        ahead = jnp.zeros_like(total)
        for d in (1, 3, 2):
            at_x, at_y = turn(x, -d), turn(y, -d)
            arrived(got1.at[0, at_x], pre_recv.at[t, d - 1])
            value = got1[0, at_x]
            total += value
            partial += jnp.where(before(at_x, x), value, 0.0)
            arrived(got1.at[1, at_y], pre_recv.at[t, 2 + d])
            ahead += jnp.where(before(at_y, y), got1[1, at_y], 0.0)
        msg[0] = total
        msg[1] = ahead
        msg[2] = ahead + chip[64:]
        for d in (2, 1, 3):
            send(
                msg.at[0], got2.at[0, y],
                pre_send.at[t, 5 + d], pre_recv.at[t, 5 + d], ydev[d],
            )
            which = jnp.where(before(x, turn(x, d)), 2, 1)
            send(
                msg.at[which], got2.at[1, x],
                pre_send.at[t, 8 + d], pre_recv.at[t, 8 + d], xdev[d],
            )
        pre[:64] = partial
        pre[64:] = ahead

    def sum_three(t, before):
        _, _, _, got2, pre = sums[t]
        upper, lower = pre[:64], pre[64:]
        for d in (1, 3, 2):
            at_x, at_y = turn(x, -d), turn(y, -d)
            arrived(got2.at[0, at_y], pre_recv.at[t, 5 + d])
            upper += jnp.where(before(at_y, y), got2[0, at_y], 0.0)
            arrived(got2.at[1, at_x], pre_recv.at[t, 8 + d])
            lower += got2[1, at_x]
        pre[:64] = upper
        pre[64:] = lower

    def result(t):
        return split(sums[t][4][...])

    def cut(a, rows):
        return a[0][rows], a[1][rows]

    earlier = lambda a, b: a < b
    later = lambda a, b: a > b

    def copies():
        yield from (
            pltpu.make_async_copy(source(s, k), w.at[s, y, x, half_rows(k)], local_sem.at[s])
            for s in range(6)
        )
        yield from (
            pltpu.make_async_copy(
                tok_ref.at[:, pl.ds(256 * c, 256)], tok(0, c), local_sem.at[6 + c]
            )
            for c in range(2)
        )

    for stage in range(3):
        give(stage)
    p1_start(0)
    p1_start(1)
    tok_start()
    p1_given(0)
    p1_given(1)
    p1_start(2)
    p1_given(2)
    for copy in copies():
        copy.start()
    for copy in copies():
        copy.wait()
    tok_share(0, 3)
    for stage in range(3):
        p1_forward(stage)
    p1_done(0)
    p2_start(0, 0)
    p2_start(0, 1)
    p1_done(1)
    p1_done(2)
    tok_forward(1)
    p2_forward(0)
    p2_start(1, 0)
    p2_start(1, 1)
    tok_forward(2)
    p2_sides(0)
    p2_done(0)
    tok_forward(3)
    tok_shared(0, 3)
    project_tokens(0, (0,), True)
    tok_shared(-1, 5)
    tok_shared(1, 6)
    project_tokens(0, (-1,))
    p2_forward(1)
    p2_start(2, 0)
    project_tokens(0, (1,))
    tok_shared(-2, 7)
    tok_shared(2, 8)
    project_tokens(0, (-2, 2))
    tok_done()
    tok_shared(-3, 9)
    tok_shared(3, 10)
    project_tokens(0, (-3, 3))
    tok_shared(4, 4)
    project_tokens(0, (4,))
    sums[0][0][...] = mm3(split(piece(KP)), split(piece(VP)), 0, 0)
    sum_one(0)
    p2_start(2, 1)
    p2_sides(1)
    project_apart(1, 0, True)
    project_apart(1, -1)
    project_apart(1, 1)
    p2_done(1)
    project_apart(1, 2)
    sums[1][0][...] = mm3(split(piece(KR)), split(piece(VR)), 0, 0)
    sum_one(1)
    p2_forward(2)
    share(KP, 0)
    share(VP, 1)
    sum_two(0, earlier)
    project_apart(2, 0, True)
    p2_sides(2)
    sum_two(1, earlier)
    project_apart(2, -1)
    project_apart(2, 1)
    p2_done(2)
    project_apart(2, 2)
    share(QP, 2)

    def causal(b):
        shape = (256, 256 * (b + 1))
        rows = lax.broadcasted_iota(jnp.int32, shape, 0) + 256 * b
        return rows >= lax.broadcasted_iota(jnp.int32, shape, 1)

    for model, (qs, ks, vs) in enumerate(((QP, KP, VP), (QR, KR, VR))):
        q, kk, v = (split(piece(s)) for s in (qs, ks, vs))
        for b in range(2):
            mine, upto = slice(256 * b, 256 * b + 256), slice(0, 256 * b + 256)
            scores = mm3(cut(q, mine), cut(kk, upto), 1, 1)
            scores = split(jnp.where(causal(b), scores, 0.0))
            att[model, mine] = mm3(scores, cut(v, upto), 1, 0)
            if model == 0:
                sc[b, 0, :, upto], sc[b, 1, :, upto] = scores
    sum_three(0, earlier)
    att[0] += mm3(split(piece(QP)), result(0), 1, 0)
    sum_three(1, earlier)
    att[1] += mm3(split(piece(QR)), result(1), 1, 0)
    ed[...] = scale * att[0] - scale * att[1]
    sums[2][0][...] = mm3(split(piece(QP)), split(ed[...]), 0, 0)
    sum_one(2)
    theirs = ed.at[core_rows(1 - k)]
    send(theirs, dgot, sib_send.at[11], sib_recv.at[11], sibling)
    diff_ref[:, lanes(k)] = ed[core_rows(k)]

    q, kk, v, e = (split(a) for a in (piece(QP), piece(KP), piece(VP), ed[...]))
    for b in range(2):
        mine, upto = slice(256 * b, 256 * b + 256), slice(0, 256 * b + 256)
        weighted = mm3(cut(e, mine), cut(v, upto), 1, 1)
        weighted = split(jnp.where(causal(b), weighted, 0.0))
        scores = sc[b, 0, :, upto], sc[b, 1, :, upto]
        dq = mm3(weighted, cut(kk, upto), 1, 0) + mm3(cut(e, mine), result(0), 1, 1)
        g[0, mine] = (scale * dq).astype(BF16)
        dk = mm3(weighted, cut(q, mine), 0, 0)
        dv = mm3(scores, cut(e, mine), 0, 0)
        if b == 0:
            att[0, upto], att[1, upto] = dk, dv
            att[0, 256:], att[1, 256:] = jnp.zeros((2, 256, HD), F32)
            sum_two(2, later)
        else:
            att[0, upto] += dk
            att[1, upto] += dv
    send(g.at[0, core_rows(1 - k)], gx.at[0], sib_send.at[12], sib_recv.at[12], sibling)
    for at_n in range(3):
        arrived(w2.at[at_n], sib_recv.at[at_n])
    sum_three(2, later)
    suffix = result(2)
    g[1] = (scale * (att[0] + mm3(split(piece(VP)), suffix, 1, 1))).astype(BF16)
    g[2] = (scale * (att[1] + mm3(split(piece(KP)), suffix, 1, 0))).astype(BF16)
    theirs = g.at[pl.ds(1, 2), core_rows(1 - k)]
    send(theirs, gx.at[pl.ds(1, 2)], sib_send.at[13], sib_recv.at[13], sibling)
    arrived(gx.at[0], sib_recv.at[12])
    arrived(gx.at[pl.ds(1, 2)], sib_recv.at[13])

    def term(by, half):
        h, few = zb(by), slice(128 * half, 128 * half + 128)
        own = pl.ds(pl.multiple_of(256 * k + 128 * half, 128), 128)
        at_h = (h // 2, pl.ds(2 * lax.rem(h, 2), 2))

        def beside(left, right):
            return jnp.concatenate([left, right], 1)

        def rows_of(ref, at_s):
            return ref[at_s, *at_h].reshape(512, HD)

        return (
            mm(beside(g[1, own], g[2, own]), beside(rows_of(w, KP), rows_of(w, VP)), 1, 1)
            + mm(beside(gx[1, few], gx[2, few]), beside(rows_of(w2, 0), rows_of(w2, 1)), 1, 1)
            + mm(beside(g[0, own], gx[0, few]), beside(rows_of(w, QP), rows_of(w2, 2)), 1, 1)
        )

    def hop(n, sign, out, inn, to, step, half):
        value = term(sign * (5 - step), half)
        fresh = step == 1 or (step == 2 and half != n)
        if not fresh:
            arrived(inn.at[step - 2, half], rs_recv.at[n, step - 2, half])
            value = value + inn[step - 2, half].astype(F32)
        out[step - 1, half] = value.astype(BF16)
        send(
            out.at[step - 1, half], inn.at[step - 1, half],
            rs_send.at[n, step - 1, half], rs_recv.at[n, step - 1, half], to,
        )

    ways = ((0, 1, out_r, in_r, zr), (1, -1, out_l, in_l, zl))
    for step in range(1, 5):
        for turn_at in range(2):
            for n, sign, out, inn, to in ways:
                half = (1 - n) if turn_at == 0 else n
                if step == 1 and half != n:
                    continue
                hop(n, sign, out, inn, to, step, half)
    for half in range(2):
        few = slice(128 * half, 128 * half + 128)
        grad_ref[few] = term(0, half)
    for turn_at in range(2):
        for n, _, _, inn, _ in ways:
            half = (1 - n) if turn_at == 0 else n
            few = slice(128 * half, 128 * half + 128)
            arrived(inn.at[3, half], rs_recv.at[n, 3, half])
            grad_ref[few] += inn[3, half].astype(F32)
    arrived(dgot, sib_recv.at[11])
    diff_ref[:, lanes(1 - k)] = dgot[...]
    for copy in sent:
        copy.wait_send()


def per_device(tokens, policy_weight, reference_weight):
    seq = tokens.shape[0] * lax.axis_size("ctx")
    scale = 1.0 / math.sqrt(HD * seq)

    whole = pltpu.VMEM((HD, HD), F32)
    some = lambda *lead: pltpu.VMEM((*lead, HD // 2, HD), F32)
    sums = (whole, some(2, 4), some(3), some(2, 4), whole)
    half = pltpu.VMEM((4, 2, 128, 512), BF16)
    dma = pltpu.SemaphoreType.DMA
    return pl.pallas_call(
        functools.partial(kernel, scale),
        out_shape=(
            pltpu.VMEM((256, 256), F32),
            pltpu.VMEM((256, 512), F32),
        ),
        in_specs=[pl.BlockSpec(memory_space=pl.ANY)] * 3,
        out_specs=[pl.BlockSpec(memory_space=pltpu.VMEM)] * 2,
        scratch_shapes=[
            pltpu.VMEM((6, 4, 4, 256, HD), BF16),
            pltpu.VMEM((3, 4, 4, 256, HD), BF16),
            pltpu.VMEM((16, 512, 256), BF16),
            pltpu.VMEM((3, 512, 2 * HD), F32),
            pltpu.VMEM((2, 512, HD), F32),
            pltpu.VMEM((2, 2, 256, 512), BF16),
            pltpu.VMEM((512, HD), F32),
            pltpu.VMEM((256, HD), F32),
            pltpu.VMEM((3, 512, HD), BF16),
            pltpu.VMEM((3, 256, HD), BF16),
            (sums, sums, sums),
            half, half, half, half,
            dma((8,)), dma((6,)), dma((6,)), dma((6, 6)), dma((6, 6)), dma((6, 6)), dma((6, 6)),
            dma((14,)), dma((14,)), dma((2, 4, 2)), dma((2, 4, 2)), dma((3, 12)), dma((3, 12)),
            dma((2, 4, 2)), dma((2, 4, 2)),
        ],
        compiler_params=pltpu.CompilerParams(
            collective_id=0, has_side_effects=True, vmem_limit_bytes=58 * 2**20
        ),
    )(tokens, policy_weight, reference_weight)


def solution(mesh):
    in_specs = (P("ctx", "head"), P(None, "ctx", "head"), P(None, "ctx", "head"))
    out_specs = (P("ctx", "head"), P("ctx", "head"))
    return jax.shard_map(
        per_device, mesh=mesh, in_specs=in_specs, out_specs=out_specs, check_vma=False
    )
```

```python
import functools
import math

import jax
import jax.numpy as jnp
from jax import lax
from jax.experimental import pallas as pl
from jax.experimental.pallas import tpu as pltpu
from jax.sharding import PartitionSpec as P

HD = 128
F32 = jnp.float32
BF16 = jnp.bfloat16
MESH = pl.DeviceIdType.MESH

PIECES = ((0, 1), (0, 2), (1, 1), (1, 2), (0, 0), (1, 0))
KP, VP, KR, VR, QP, QR = range(6)


def mm(a, b, ca, cb):
    return lax.dot_general(a, b, (((ca,), (cb,)), ((), ())), preferred_element_type=F32)


def split(a):
    high = a.astype(BF16)
    return high, (a - high.astype(F32)).astype(BF16)


def mm3(a, b, ca, cb):
    return mm(a[0], b[0], ca, cb) + (mm(a[0], b[1], ca, cb) + mm(a[1], b[0], ca, cb))


def kernel(
    scale, tok_ref, pol_ref, ref_ref, diff_ref, grad_ref,
    w, w2, given_away, xs, acc, att, sc, ed, dgot, g, gx, sums,
    out_r, in_r, out_l, in_l,
    local_sem, give_send, give_recv, p1_send, p1_recv, p2_send, p2_recv, sib_send, sib_recv,
    tok_send, tok_recv, pre_send, pre_recv, rs_send, rs_recv,
):
    ctx, z = lax.axis_index("ctx"), lax.axis_index("head")
    y, x, k = ctx // 8, lax.rem(ctx // 2, 4), lax.rem(ctx, 2)
    zs = lax.axis_size("head")

    def at(yy, xx, kk):
        return ((yy * 4 + xx) * 2 + kk, z)

    def turn(i, by):
        return lax.rem(i + by + 4, 4)

    xdev = [at(y, turn(x, d), k) for d in range(4)]
    ydev = [at(turn(y, d), x, k) for d in range(4)]
    sibling = at(y, x, 1 - k)
    zr, zl = (ctx, lax.rem(z + 1, zs)), (ctx, lax.rem(z + zs - 1, zs))

    def zb(by):
        return lax.rem(z + by + zs, zs)

    sent = []

    def send(src, dst, ssem, rsem, dev):
        copy = pltpu.make_async_remote_copy(
            src_ref=src, dst_ref=dst, send_sem=ssem, recv_sem=rsem,
            device_id=dev, device_id_type=MESH,
        )
        copy.start()
        sent.append(copy)

    def arrived(dst, sem):
        pltpu.make_async_remote_copy(
            src_ref=dst, dst_ref=dst, send_sem=sem, recv_sem=sem,
            device_id=sibling, device_id_type=MESH,
        ).wait_recv()

    def lanes(kk):
        return pl.ds(pl.multiple_of(HD * kk, HD), HD)

    def half_rows(p):
        return pl.ds(pl.multiple_of(128 * p, 128), 128)

    def core_rows(kk):
        return pl.ds(pl.multiple_of(256 * kk, 256), 256)

    def source(s, kk):
        model, slot = PIECES[s]
        return (pol_ref, ref_ref)[model].at[slot, :, lanes(kk)]

    def block(s, i, j):
        return w.at[s, j, i] if s % 2 == 0 else w.at[s, i, j]

    def part(s, i, j, p):
        rows = half_rows(p)
        return w.at[s, j, i, rows] if s % 2 == 0 else w.at[s, i, j, rows]

    def some(s, j, half):
        few = pl.ds(2 * half, 2)
        return w.at[s, j, few] if s % 2 == 0 else w.at[s, few, j]

    def axes(s):
        return (x, y, xdev, ydev) if s % 2 == 0 else (y, x, ydev, xdev)

    def pair(stage):
        return (2 * stage, 2 * stage + 1)

    def give(stage):
        for s in pair(stage):
            send(
                given_away.at[s], w.at[s, y, x, half_rows(k)],
                give_send.at[s], give_recv.at[s], sibling,
            )

    def p1_start(stage):
        for s in pair(stage):
            i, j, first, _ = axes(s)
            for n, d in ((0, 1), (1, 3)):
                at_n = 2 * n + k
                send(
                    part(s, i, j, k), part(s, i, j, k),
                    p1_send.at[s, at_n], p1_recv.at[s, at_n], first[d],
                )

    def p1_given(stage):
        for s in pair(stage):
            i, j, first, _ = axes(s)
            given = part(s, i, j, 1 - k)
            arrived(given, give_recv.at[s])
            for n, d in ((0, 1), (1, 3)):
                at_n = 2 * n + 1 - k
                send(given, given, p1_send.at[s, at_n], p1_recv.at[s, at_n], first[d])

    def p1_forward(stage):
        for n, d, to in ((0, -1, 1), (1, 1, 3)):
            for s in pair(stage):
                i, j, first, _ = axes(s)
                half = part(s, turn(i, d), j, n)
                arrived(half, p1_recv.at[s, 3 * n])
                send(half, half, p1_send.at[s, 4 + n], p1_recv.at[s, 4 + n], first[to])

    def p1_done(stage):
        for s in pair(stage):
            i, j, _, _ = axes(s)
            for n, d in ((0, -1), (1, 1)):
                arrived(part(s, turn(i, d), j, 1 - n), p1_recv.at[s, 1 + n])
            for n in range(2):
                arrived(part(s, turn(i, 2), j, n), p1_recv.at[s, 4 + n])

    def p2_start(stage, second_half):
        for s in pair(stage):
            _, j, _, second = axes(s)
            for n, d in ((0, 1), (1, 3)):
                mine = some(s, j, n ^ second_half)
                at_n = 2 * n + second_half
                send(mine, mine, p2_send.at[s, at_n], p2_recv.at[s, at_n], second[d])

    def p2_forward(stage):
        for n, d, to in ((0, -1, 1), (1, 1, 3)):
            for s in pair(stage):
                _, j, _, second = axes(s)
                half = some(s, turn(j, d), n)
                arrived(half, p2_recv.at[s, 2 * n])
                send(half, half, p2_send.at[s, 4 + n], p2_recv.at[s, 4 + n], second[to])

    def p2_sides(stage):
        for n, d in ((0, -1), (1, 1)):
            for s in pair(stage):
                arrived(some(s, turn(axes(s)[1], d), 1 - n), p2_recv.at[s, 2 * n + 1])

    def p2_done(stage):
        for n in range(2):
            for s in pair(stage):
                arrived(some(s, turn(axes(s)[1], 2), n), p2_recv.at[s, 4 + n])

    def share(s, at_n):
        send(w.at[s], w2.at[at_n], sib_send.at[at_n], sib_recv.at[at_n], sibling)

    def tok(by, c):
        return xs.at[2 * zb(by) + c, core_rows(k)]

    def tok_both(by, kk):
        return xs.at[pl.ds(2 * zb(by), 2), core_rows(kk)]

    def tok_share(by, at_n):
        mine = tok_both(by, k)
        send(mine, mine, sib_send.at[at_n], sib_recv.at[at_n], sibling)

    def tok_shared(by, at_n):
        arrived(tok_both(by, 1 - k), sib_recv.at[at_n])

    def tok_start():
        for c in range(2):
            for n, to in ((0, zr), (1, zl)):
                cc = c ^ n
                send(tok(0, cc), tok(0, cc), tok_send.at[n, 0, cc], tok_recv.at[n, 0, cc], to)

    def tok_forward(step):
        for c in range(2):
            for n, by, to in ((0, -step, zr), (1, step, zl)):
                cc = c ^ n
                arrived(tok(by, cc), tok_recv.at[n, step - 1, cc])
                if step < 3 or c == 0:
                    send(
                        tok(by, cc), tok(by, cc),
                        tok_send.at[n, step, cc], tok_recv.at[n, step, cc], to,
                    )
        tok_share(-step, 3 + 2 * step)
        tok_share(step, 4 + 2 * step)

    def tok_done():
        for n in range(2):
            arrived(tok(4, n), tok_recv.at[n, 3, n])
        tok_share(4, 4)

    def both(ref, first, second, f):
        at_f = (f // 4, lax.rem(f, 4))
        return jnp.concatenate([ref[first, *at_f], ref[second, *at_f]], 1)

    def add_chunks(stage, chunks, first):
        total = acc[stage] if not first else None
        for f in chunks:
            value = mm(xs[f], both(w, *pair(stage), f), 1, 0)
            total = value if total is None else total + value
        acc[stage] = total

    def project_tokens(stage, places, first=False):
        add_chunks(stage, [2 * zb(by) + c for by in places for c in range(2)], first)

    def project_places(stage, places, first=False):
        add_chunks(stage, [4 * turn(y, dy) + turn(x, dx) for dy, dx in places], first)

    near = [(dy, dx) for dy in (0, -1, 1) for dx in (0, -1, 1)]
    far = [(2, dx) for dx in (0, -1, 1, 2)] + [(dy, 2) for dy in (0, -1, 1)]

    def piece(s):
        return acc[s // 2, :, (s % 2) * HD:(s % 2 + 1) * HD]

    up, low = pl.ds(0, 64), pl.ds(64, 64)

    def sum_one(t):
        chip, got1 = sums[t][:2]
        for d in (2, 1, 3):
            for q, devs, i, few in ((0, xdev, x, up), (1, ydev, y, low)):
                at_n = 3 * q + d - 1
                send(
                    chip.at[few], got1.at[q, i],
                    pre_send.at[t, at_n], pre_recv.at[t, at_n], devs[d],
                )

    def sum_two(t, before):
        chip, got1, msg, got2, pre = sums[t]
        total = chip[:64]
        partial = jnp.zeros_like(total)
        ahead = jnp.zeros_like(total)
        for d in (1, 3, 2):
            at_x, at_y = turn(x, -d), turn(y, -d)
            arrived(got1.at[0, at_x], pre_recv.at[t, d - 1])
            value = got1[0, at_x]
            total += value
            partial += jnp.where(before(at_x, x), value, 0.0)
            arrived(got1.at[1, at_y], pre_recv.at[t, 2 + d])
            ahead += jnp.where(before(at_y, y), got1[1, at_y], 0.0)
        msg[0] = total
        msg[1] = ahead
        msg[2] = ahead + chip[64:]
        for d in (2, 1, 3):
            send(
                msg.at[0], got2.at[0, y],
                pre_send.at[t, 5 + d], pre_recv.at[t, 5 + d], ydev[d],
            )
            which = jnp.where(before(x, turn(x, d)), 2, 1)
            send(
                msg.at[which], got2.at[1, x],
                pre_send.at[t, 8 + d], pre_recv.at[t, 8 + d], xdev[d],
            )
        pre[:64] = partial
        pre[64:] = ahead

    def sum_three(t, before):
        _, _, _, got2, pre = sums[t]
        upper, lower = pre[:64], pre[64:]
        for d in (1, 3, 2):
            at_x, at_y = turn(x, -d), turn(y, -d)
            arrived(got2.at[0, at_y], pre_recv.at[t, 5 + d])
            upper += jnp.where(before(at_y, y), got2[0, at_y], 0.0)
            arrived(got2.at[1, at_x], pre_recv.at[t, 8 + d])
            lower += got2[1, at_x]
        pre[:64] = upper
        pre[64:] = lower

    def result(t):
        return split(sums[t][4][...])

    def cut(a, rows):
        return a[0][rows], a[1][rows]

    earlier = lambda a, b: a < b
    later = lambda a, b: a > b

    def copies():
        yield from (
            pltpu.make_async_copy(source(s, k), w.at[s, y, x, half_rows(k)], local_sem.at[s])
            for s in range(6)
        )
        yield from (
            pltpu.make_async_copy(source(s, 1 - k), given_away.at[s], local_sem.at[8 + s])
            for s in range(6)
        )
        yield from (
            pltpu.make_async_copy(
                tok_ref.at[:, pl.ds(256 * c, 256)], tok(0, c), local_sem.at[6 + c]
            )
            for c in range(2)
        )

    for copy in copies():
        copy.start()
    barrier = pltpu.get_barrier_semaphore()
    greeted = xdev[1:] + ydev[1:] + [sibling, zr, zl]
    for dev in greeted:
        pl.semaphore_signal(barrier, inc=1, device_id=dev, device_id_type=MESH)
    pl.semaphore_wait(barrier, len(greeted))

    for copy in copies():
        copy.wait()
    for stage in range(3):
        give(stage)
    p1_start(0)
    p1_start(1)
    tok_start()
    p1_given(0)
    p1_given(1)
    p1_start(2)
    p1_given(2)
    tok_share(0, 3)
    for stage in range(3):
        p1_forward(stage)
    p1_done(0)
    p2_start(0, 0)
    p2_start(0, 1)
    p1_done(1)
    p1_done(2)
    tok_forward(1)
    p2_forward(0)
    p2_start(1, 0)
    p2_start(1, 1)
    tok_forward(2)
    p2_sides(0)
    p2_done(0)
    tok_shared(0, 3)
    project_tokens(0, (0,), True)
    tok_forward(3)
    p2_forward(1)
    p2_start(2, 0)
    tok_shared(-1, 5)
    tok_shared(1, 6)
    project_tokens(0, (-1,))
    project_tokens(0, (1,))
    tok_shared(-2, 7)
    tok_shared(2, 8)
    project_tokens(0, (-2, 2))
    tok_done()
    tok_shared(-3, 9)
    tok_shared(3, 10)
    project_tokens(0, (-3, 3))
    tok_shared(4, 4)
    project_tokens(0, (4,))
    sums[0][0][...] = mm3(split(piece(KP)), split(piece(VP)), 0, 0)
    sum_one(0)
    p2_start(2, 1)
    p2_sides(1)
    project_places(1, near, True)
    p2_done(1)
    project_places(1, far)
    sums[1][0][...] = mm3(split(piece(KR)), split(piece(VR)), 0, 0)
    sum_one(1)
    p2_forward(2)
    share(KP, 0)
    share(VP, 1)
    sum_two(0, earlier)
    p2_sides(2)
    project_places(2, near, True)
    sum_two(1, earlier)
    p2_done(2)
    project_places(2, far)
    share(QP, 2)

    def causal(b):
        shape = (256, 256 * (b + 1))
        rows = lax.broadcasted_iota(jnp.int32, shape, 0) + 256 * b
        return rows >= lax.broadcasted_iota(jnp.int32, shape, 1)

    spans = [(slice(256 * b, 256 * b + 256), slice(0, 256 * b + 256)) for b in range(2)]
    inner = {}
    for model, (qs, ks) in enumerate(((QP, KP), (QR, KR))):
        q, kk = split(piece(qs)), split(piece(ks))
        for b, (mine, upto) in enumerate(spans):
            scores = mm3(cut(q, mine), cut(kk, upto), 1, 1)
            inner[model, b] = split(jnp.where(causal(b), scores, 0.0))
    for model, vs in enumerate((VP, VR)):
        v = split(piece(vs))
        for b, (mine, upto) in enumerate(spans):
            att[model, mine] = mm3(inner[model, b], cut(v, upto), 1, 0)
    for b, (_, upto) in enumerate(spans):
        sc[b, 0, :, upto], sc[b, 1, :, upto] = inner[0, b]
    sum_three(0, earlier)
    att[0] += mm3(split(piece(QP)), result(0), 1, 0)
    sum_three(1, earlier)
    att[1] += mm3(split(piece(QR)), result(1), 1, 0)
    ed[...] = scale * att[0] - scale * att[1]
    sums[2][0][...] = mm3(split(piece(QP)), split(ed[...]), 0, 0)
    sum_one(2)
    theirs = ed.at[core_rows(1 - k)]
    send(theirs, dgot, sib_send.at[11], sib_recv.at[11], sibling)
    diff_ref[:, lanes(k)] = ed[core_rows(k)]

    q, kk, v, e = (split(a) for a in (piece(QP), piece(KP), piece(VP), ed[...]))
    for b, (mine, upto) in enumerate(spans):
        weighted = mm3(cut(e, mine), cut(v, upto), 1, 1)
        weighted = split(jnp.where(causal(b), weighted, 0.0))
        scores = sc[b, 0, :, upto], sc[b, 1, :, upto]
        dq = mm3(weighted, cut(kk, upto), 1, 0) + mm3(cut(e, mine), result(0), 1, 1)
        g[0, mine] = (scale * dq).astype(BF16)
        dk = mm3(weighted, cut(q, mine), 0, 0)
        dv = mm3(scores, cut(e, mine), 0, 0)
        if b == 0:
            att[0, upto], att[1, upto] = dk, dv
            att[0, 256:], att[1, 256:] = jnp.zeros((2, 256, HD), F32)
            sum_two(2, later)
        else:
            att[0, upto] += dk
            att[1, upto] += dv
    send(g.at[0, core_rows(1 - k)], gx.at[0], sib_send.at[12], sib_recv.at[12], sibling)
    for at_n in range(3):
        arrived(w2.at[at_n], sib_recv.at[at_n])
    sum_three(2, later)
    suffix = result(2)

    def finish(kk):
        rows = core_rows(kk)
        keys, values = split(acc[0, rows, :HD]), split(acc[0, rows, HD:])
        g[1, rows] = (scale * (att[0, rows] + mm3(values, suffix, 1, 1))).astype(BF16)
        g[2, rows] = (scale * (att[1, rows] + mm3(keys, suffix, 1, 0))).astype(BF16)

    finish(1 - k)
    theirs = g.at[pl.ds(1, 2), core_rows(1 - k)]
    send(theirs, gx.at[pl.ds(1, 2)], sib_send.at[13], sib_recv.at[13], sibling)
    finish(k)
    arrived(gx.at[0], sib_recv.at[12])

    def beside(left, right):
        return jnp.concatenate([left, right], 1)

    def rows_of(ref, at_s, h):
        return ref[at_s, h // 2, pl.ds(2 * lax.rem(h, 2), 2)].reshape(512, HD)

    def own_term(by, start, size):
        h, few = zb(by), pl.ds(start, size)
        own = pl.ds(pl.multiple_of(256 * k + start, 128), size)
        return (
            mm(beside(g[1, own], g[2, own]), beside(rows_of(w, KP, h), rows_of(w, VP, h)), 1, 1)
            + mm(beside(g[0, own], gx[0, few]), beside(rows_of(w, QP, h), rows_of(w2, 2, h)), 1, 1)
        )

    def other_term(by, start, size):
        h, few = zb(by), pl.ds(start, size)
        return mm(beside(gx[1, few], gx[2, few]), beside(rows_of(w2, 0, h), rows_of(w2, 1, h)), 1, 1)

    def term(by, half):
        return own_term(by, 128 * half, 128) + other_term(by, 128 * half, 128)

    opposite = own_term(4, 0, 256)
    arrived(gx.at[pl.ds(1, 2)], sib_recv.at[13])
    opposite = opposite + other_term(4, 0, 256)

    def hop(n, sign, out, inn, to, step, half):
        if step == 1:
            value = opposite[128 * half:128 * half + 128]
        else:
            value = term(sign * (5 - step), half)
        fresh = step == 1 or (step == 2 and half != n)
        if not fresh:
            arrived(inn.at[step - 2, half], rs_recv.at[n, step - 2, half])
            value = value + inn[step - 2, half].astype(F32)
        out[step - 1, half] = value.astype(BF16)
        send(
            out.at[step - 1, half], inn.at[step - 1, half],
            rs_send.at[n, step - 1, half], rs_recv.at[n, step - 1, half], to,
        )

    ways = ((0, 1, out_r, in_r, zr), (1, -1, out_l, in_l, zl))
    for step in range(1, 5):
        for turn_at in range(2):
            for n, sign, out, inn, to in ways:
                half = (1 - n) if turn_at == 0 else n
                if step == 1 and half != n:
                    continue
                hop(n, sign, out, inn, to, step, half)
    grad_ref[...] = own_term(0, 0, 256) + other_term(0, 0, 256)
    for turn_at in range(2):
        for n, _, _, inn, _ in ways:
            half = (1 - n) if turn_at == 0 else n
            few = slice(128 * half, 128 * half + 128)
            arrived(inn.at[3, half], rs_recv.at[n, 3, half])
            grad_ref[few] += inn[3, half].astype(F32)
    arrived(dgot, sib_recv.at[11])
    diff_ref[:, lanes(1 - k)] = dgot[...]
    for copy in sent:
        copy.wait_send()


def per_device(tokens, policy_weight, reference_weight):
    seq = tokens.shape[0] * lax.axis_size("ctx")
    scale = 1.0 / math.sqrt(HD * seq)

    whole = pltpu.VMEM((HD, HD), F32)
    some = lambda *lead: pltpu.VMEM((*lead, HD // 2, HD), F32)
    sums = (whole, some(2, 4), some(3), some(2, 4), whole)
    half = pltpu.VMEM((4, 2, 128, 512), BF16)
    dma = pltpu.SemaphoreType.DMA
    return pl.pallas_call(
        functools.partial(kernel, scale),
        out_shape=(
            pltpu.VMEM((256, 256), F32),
            pltpu.VMEM((256, 512), F32),
        ),
        in_specs=[pl.BlockSpec(memory_space=pl.ANY)] * 3,
        out_specs=[pl.BlockSpec(memory_space=pltpu.VMEM)] * 2,
        scratch_shapes=[
            pltpu.VMEM((6, 4, 4, 256, HD), BF16),
            pltpu.VMEM((3, 4, 4, 256, HD), BF16),
            pltpu.VMEM((6, 128, HD), BF16),
            pltpu.VMEM((16, 512, 256), BF16),
            pltpu.VMEM((3, 512, 2 * HD), F32),
            pltpu.VMEM((2, 512, HD), F32),
            pltpu.VMEM((2, 2, 256, 512), BF16),
            pltpu.VMEM((512, HD), F32),
            pltpu.VMEM((256, HD), F32),
            pltpu.VMEM((3, 512, HD), BF16),
            pltpu.VMEM((3, 256, HD), BF16),
            (sums, sums, sums),
            half, half, half, half,
            dma((14,)), dma((6,)), dma((6,)), dma((6, 6)), dma((6, 6)), dma((6, 6)), dma((6, 6)),
            dma((14,)), dma((14,)), dma((2, 4, 2)), dma((2, 4, 2)), dma((3, 12)), dma((3, 12)),
            dma((2, 4, 2)), dma((2, 4, 2)),
        ],
        compiler_params=pltpu.CompilerParams(
            collective_id=0, has_side_effects=True, vmem_limit_bytes=58 * 2**20
        ),
    )(tokens, policy_weight, reference_weight)


def solution(mesh):
    in_specs = (P("ctx", "head"), P(None, "ctx", "head"), P(None, "ctx", "head"))
    out_specs = (P("ctx", "head"), P("ctx", "head"))
    return jax.shard_map(
        per_device, mesh=mesh, in_specs=in_specs, out_specs=out_specs, check_vma=False
    )
```

```python
import functools
import math

import jax
import jax.numpy as jnp
from jax import lax
from jax.experimental import pallas as pl
from jax.experimental.pallas import tpu as pltpu
from jax.sharding import PartitionSpec as P

HD = 128
F32 = jnp.float32
BF16 = jnp.bfloat16
MESH = pl.DeviceIdType.MESH

PIECES = ((0, 1), (0, 2), (1, 1), (1, 2), (0, 0), (1, 0))
KP, VP, KR, VR, QP, QR = range(6)


def mm(a, b, ca, cb):
    return lax.dot_general(a, b, (((ca,), (cb,)), ((), ())), preferred_element_type=F32)


def split(a):
    high = a.astype(BF16)
    return high, (a - high.astype(F32)).astype(BF16)


def mm3(a, b, ca, cb):
    return mm(a[0], b[0], ca, cb) + (mm(a[0], b[1], ca, cb) + mm(a[1], b[0], ca, cb))


def kernel(
    scale, tok_ref, pol_ref, ref_ref, diff_ref, grad_ref,
    w, w2, given_away, xs, acc, att, sc, ed, dgot, g, gx, sums,
    out_r, in_r, out_l, in_l,
    local_sem, give_send, give_recv, p1_send, p1_recv, p2_send, p2_recv, sib_send, sib_recv,
    tok_send, tok_recv, pre_send, pre_recv, rs_send, rs_recv,
):
    ctx, z = lax.axis_index("ctx"), lax.axis_index("head")
    y, x, k = ctx // 8, lax.rem(ctx // 2, 4), lax.rem(ctx, 2)
    zs = lax.axis_size("head")

    def at(yy, xx, kk):
        return ((yy * 4 + xx) * 2 + kk, z)

    def turn(i, by):
        return lax.rem(i + by + 4, 4)

    xdev = [at(y, turn(x, d), k) for d in range(4)]
    ydev = [at(turn(y, d), x, k) for d in range(4)]
    sibling = at(y, x, 1 - k)
    zr, zl = (ctx, lax.rem(z + 1, zs)), (ctx, lax.rem(z + zs - 1, zs))

    def zb(by):
        return lax.rem(z + by + zs, zs)

    sent = []

    def send(src, dst, ssem, rsem, dev):
        copy = pltpu.make_async_remote_copy(
            src_ref=src, dst_ref=dst, send_sem=ssem, recv_sem=rsem,
            device_id=dev, device_id_type=MESH,
        )
        copy.start()
        sent.append(copy)

    def arrived(dst, sem):
        pltpu.make_async_remote_copy(
            src_ref=dst, dst_ref=dst, send_sem=sem, recv_sem=sem,
            device_id=sibling, device_id_type=MESH,
        ).wait_recv()

    def lanes(kk):
        return pl.ds(pl.multiple_of(HD * kk, HD), HD)

    def half_rows(p):
        return pl.ds(pl.multiple_of(128 * p, 128), 128)

    def core_rows(kk):
        return pl.ds(pl.multiple_of(256 * kk, 256), 256)

    def source(s, kk):
        model, slot = PIECES[s]
        return (pol_ref, ref_ref)[model].at[slot, :, lanes(kk)]

    def block(s, i, j):
        return w.at[s, j, i] if s % 2 == 0 else w.at[s, i, j]

    def part(s, i, j, p):
        rows = half_rows(p)
        return w.at[s, j, i, rows] if s % 2 == 0 else w.at[s, i, j, rows]

    def some(s, j, half):
        few = pl.ds(2 * half, 2)
        return w.at[s, j, few] if s % 2 == 0 else w.at[s, few, j]

    def axes(s):
        return (x, y, xdev, ydev) if s % 2 == 0 else (y, x, ydev, xdev)

    def pair(stage):
        return (2 * stage, 2 * stage + 1)

    def give(stage):
        for s in pair(stage):
            send(
                given_away.at[s], w.at[s, y, x, half_rows(k)],
                give_send.at[s], give_recv.at[s], sibling,
            )

    def p1_start(stage):
        for s in pair(stage):
            i, j, first, _ = axes(s)
            for n, d in ((0, 1), (1, 3)):
                at_n = 2 * n + k
                send(
                    part(s, i, j, k), part(s, i, j, k),
                    p1_send.at[s, at_n], p1_recv.at[s, at_n], first[d],
                )

    def p1_given(stage):
        for s in pair(stage):
            i, j, first, _ = axes(s)
            given = part(s, i, j, 1 - k)
            arrived(given, give_recv.at[s])
            for n, d in ((0, 1), (1, 3)):
                at_n = 2 * n + 1 - k
                send(given, given, p1_send.at[s, at_n], p1_recv.at[s, at_n], first[d])

    def p1_forward(stage):
        for n, d, to in ((0, -1, 1), (1, 1, 3)):
            for s in pair(stage):
                i, j, first, _ = axes(s)
                half = part(s, turn(i, d), j, n)
                arrived(half, p1_recv.at[s, 3 * n])
                send(half, half, p1_send.at[s, 4 + n], p1_recv.at[s, 4 + n], first[to])

    def p1_done(stage):
        for s in pair(stage):
            i, j, _, _ = axes(s)
            for n, d in ((0, -1), (1, 1)):
                arrived(part(s, turn(i, d), j, 1 - n), p1_recv.at[s, 1 + n])
            for n in range(2):
                arrived(part(s, turn(i, 2), j, n), p1_recv.at[s, 4 + n])

    def p2_start(stage, second_half):
        for s in pair(stage):
            _, j, _, second = axes(s)
            for n, d in ((0, 1), (1, 3)):
                mine = some(s, j, n ^ second_half)
                at_n = 2 * n + second_half
                send(mine, mine, p2_send.at[s, at_n], p2_recv.at[s, at_n], second[d])

    def p2_forward(stage):
        for n, d, to in ((0, -1, 1), (1, 1, 3)):
            for s in pair(stage):
                _, j, _, second = axes(s)
                half = some(s, turn(j, d), n)
                arrived(half, p2_recv.at[s, 2 * n])
                send(half, half, p2_send.at[s, 4 + n], p2_recv.at[s, 4 + n], second[to])

    def p2_sides(stage):
        for n, d in ((0, -1), (1, 1)):
            for s in pair(stage):
                arrived(some(s, turn(axes(s)[1], d), 1 - n), p2_recv.at[s, 2 * n + 1])

    def p2_done(stage):
        for n in range(2):
            for s in pair(stage):
                arrived(some(s, turn(axes(s)[1], 2), n), p2_recv.at[s, 4 + n])

    def share(s, at_n):
        send(w.at[s], w2.at[at_n], sib_send.at[at_n], sib_recv.at[at_n], sibling)

    def tok(by, c):
        return xs.at[2 * zb(by) + c, core_rows(k)]

    def tok_both(by, kk):
        return xs.at[pl.ds(2 * zb(by), 2), core_rows(kk)]

    def tok_share(by, at_n):
        mine = tok_both(by, k)
        send(mine, mine, sib_send.at[at_n], sib_recv.at[at_n], sibling)

    def tok_shared(by, at_n):
        arrived(tok_both(by, 1 - k), sib_recv.at[at_n])

    def tok_start():
        for c in range(2):
            for n, to in ((0, zr), (1, zl)):
                cc = c ^ n
                send(tok(0, cc), tok(0, cc), tok_send.at[n, 0, cc], tok_recv.at[n, 0, cc], to)

    def tok_forward(step):
        for c in range(2):
            for n, by, to in ((0, -step, zr), (1, step, zl)):
                cc = c ^ n
                arrived(tok(by, cc), tok_recv.at[n, step - 1, cc])
                if step < 3 or c == 0:
                    send(
                        tok(by, cc), tok(by, cc),
                        tok_send.at[n, step, cc], tok_recv.at[n, step, cc], to,
                    )
        tok_share(-step, 3 + 2 * step)
        tok_share(step, 4 + 2 * step)

    def tok_done():
        for n in range(2):
            arrived(tok(4, n), tok_recv.at[n, 3, n])
        tok_share(4, 4)

    def both(ref, first, second, f):
        at_f = (f // 4, lax.rem(f, 4))
        return jnp.concatenate([ref[first, *at_f], ref[second, *at_f]], 1)

    def add_chunks(stage, chunks, first):
        total = acc[stage] if not first else None
        for f in chunks:
            value = mm(xs[f], both(w, *pair(stage), f), 1, 0)
            total = value if total is None else total + value
        acc[stage] = total

    def project_tokens(stage, places, first=False):
        add_chunks(stage, [2 * zb(by) + c for by in places for c in range(2)], first)

    def project_places(stage, places, first=False):
        add_chunks(stage, [4 * turn(y, dy) + turn(x, dx) for dy, dx in places], first)

    near = [(dy, dx) for dy in (0, -1, 1) for dx in (0, -1, 1)]
    far = [(2, dx) for dx in (0, -1, 1, 2)] + [(dy, 2) for dy in (0, -1, 1)]

    def piece(s):
        return acc[s // 2, :, (s % 2) * HD:(s % 2 + 1) * HD]

    up, low = pl.ds(0, 64), pl.ds(64, 64)

    def sum_one(t):
        chip, got1 = sums[t][:2]
        for d in (2, 1, 3):
            for q, devs, i, few in ((0, xdev, x, up), (1, ydev, y, low)):
                at_n = 3 * q + d - 1
                send(
                    chip.at[few], got1.at[q, i],
                    pre_send.at[t, at_n], pre_recv.at[t, at_n], devs[d],
                )

    def sum_two(t, before):
        chip, got1, msg, got2, pre = sums[t]
        total = chip[:64]
        partial = jnp.zeros_like(total)
        ahead = jnp.zeros_like(total)
        for d in (1, 3, 2):
            at_x = turn(x, -d)
            arrived(got1.at[0, at_x], pre_recv.at[t, d - 1])
            value = got1[0, at_x]
            total += value
            partial += jnp.where(before(at_x, x), value, 0.0)
        msg[0] = total
        for d in (2, 1, 3):
            send(
                msg.at[0], got2.at[0, y],
                pre_send.at[t, 5 + d], pre_recv.at[t, 5 + d], ydev[d],
            )
        for d in (1, 3, 2):
            at_y = turn(y, -d)
            arrived(got1.at[1, at_y], pre_recv.at[t, 2 + d])
            ahead += jnp.where(before(at_y, y), got1[1, at_y], 0.0)
        msg[1] = ahead
        msg[2] = ahead + chip[64:]
        for d in (2, 1, 3):
            which = jnp.where(before(x, turn(x, d)), 2, 1)
            send(
                msg.at[which], got2.at[1, x],
                pre_send.at[t, 8 + d], pre_recv.at[t, 8 + d], xdev[d],
            )
        pre[:64] = partial
        pre[64:] = ahead

    def sum_three(t, before):
        _, _, _, got2, pre = sums[t]
        upper, lower = pre[:64], pre[64:]
        for d in (1, 3, 2):
            at_x, at_y = turn(x, -d), turn(y, -d)
            arrived(got2.at[0, at_y], pre_recv.at[t, 5 + d])
            upper += jnp.where(before(at_y, y), got2[0, at_y], 0.0)
            arrived(got2.at[1, at_x], pre_recv.at[t, 8 + d])
            lower += got2[1, at_x]
        pre[:64] = upper
        pre[64:] = lower

    def result(t):
        return split(sums[t][4][...])

    def cut(a, rows):
        return a[0][rows], a[1][rows]

    earlier = lambda a, b: a < b
    later = lambda a, b: a > b

    def copies():
        yield from (
            pltpu.make_async_copy(source(s, k), w.at[s, y, x, half_rows(k)], local_sem.at[s])
            for s in range(6)
        )
        yield from (
            pltpu.make_async_copy(source(s, 1 - k), given_away.at[s], local_sem.at[8 + s])
            for s in range(6)
        )
        yield from (
            pltpu.make_async_copy(
                tok_ref.at[:, pl.ds(256 * c, 256)], tok(0, c), local_sem.at[6 + c]
            )
            for c in range(2)
        )

    for copy in copies():
        copy.start()
    barrier = pltpu.get_barrier_semaphore()
    greeted = xdev[1:] + ydev[1:] + [sibling, zr, zl]
    for dev in greeted:
        pl.semaphore_signal(barrier, inc=1, device_id=dev, device_id_type=MESH)
    pl.semaphore_wait(barrier, len(greeted))

    for copy in copies():
        copy.wait()
    for stage in range(3):
        give(stage)
    p1_start(0)
    p1_start(1)
    tok_start()
    p1_given(0)
    p1_given(1)
    p1_start(2)
    p1_given(2)
    tok_share(0, 3)
    for stage in range(3):
        p1_forward(stage)
    p1_done(0)
    p2_start(0, 0)
    p2_start(0, 1)
    p1_done(1)
    p1_done(2)
    tok_forward(1)
    p2_forward(0)
    p2_start(1, 0)
    p2_start(1, 1)
    tok_forward(2)
    p2_sides(0)
    p2_done(0)
    tok_shared(0, 3)
    project_tokens(0, (0,), True)
    tok_forward(3)
    p2_forward(1)
    p2_start(2, 0)
    tok_shared(-1, 5)
    tok_shared(1, 6)
    project_tokens(0, (-1,))
    project_tokens(0, (1,))
    tok_shared(-2, 7)
    tok_shared(2, 8)
    project_tokens(0, (-2, 2))
    tok_done()
    tok_shared(-3, 9)
    tok_shared(3, 10)
    project_tokens(0, (-3, 3))
    tok_shared(4, 4)
    project_tokens(0, (4,))
    sums[0][0][...] = mm3(split(piece(KP)), split(piece(VP)), 0, 0)
    sum_one(0)
    p2_start(2, 1)
    p2_sides(1)
    project_places(1, near, True)
    p2_done(1)
    project_places(1, far)
    sums[1][0][...] = mm3(split(piece(KR)), split(piece(VR)), 0, 0)
    sum_one(1)
    p2_forward(2)
    share(KP, 0)
    share(VP, 1)
    sum_two(0, earlier)
    p2_sides(2)
    project_places(2, near, True)
    sum_two(1, earlier)
    p2_done(2)
    project_places(2, far)
    share(QP, 2)

    def causal(b):
        shape = (256, 256 * (b + 1))
        rows = lax.broadcasted_iota(jnp.int32, shape, 0) + 256 * b
        return rows >= lax.broadcasted_iota(jnp.int32, shape, 1)

    spans = [(slice(256 * b, 256 * b + 256), slice(0, 256 * b + 256)) for b in range(2)]
    inner = {}
    for model, (qs, ks) in enumerate(((QP, KP), (QR, KR))):
        q, kk = split(piece(qs)), split(piece(ks))
        for b, (mine, upto) in enumerate(spans):
            scores = mm3(cut(q, mine), cut(kk, upto), 1, 1)
            inner[model, b] = split(jnp.where(causal(b), scores, 0.0))
    for model, vs in enumerate((VP, VR)):
        v = split(piece(vs))
        for b, (mine, upto) in enumerate(spans):
            att[model, mine] = mm3(inner[model, b], cut(v, upto), 1, 0)
    for b, (_, upto) in enumerate(spans):
        sc[b, 0, :, upto], sc[b, 1, :, upto] = inner[0, b]
    sum_three(0, earlier)
    att[0] += mm3(split(piece(QP)), result(0), 1, 0)
    sum_three(1, earlier)
    att[1] += mm3(split(piece(QR)), result(1), 1, 0)
    ed[...] = scale * att[0] - scale * att[1]
    sums[2][0][...] = mm3(split(piece(QP)), split(ed[...]), 0, 0)
    sum_one(2)
    theirs = ed.at[core_rows(1 - k)]
    send(theirs, dgot, sib_send.at[11], sib_recv.at[11], sibling)
    diff_ref[:, lanes(k)] = ed[core_rows(k)]

    q, kk, v, e = (split(a) for a in (piece(QP), piece(KP), piece(VP), ed[...]))
    for b, (mine, upto) in enumerate(spans):
        weighted = mm3(cut(e, mine), cut(v, upto), 1, 1)
        weighted = split(jnp.where(causal(b), weighted, 0.0))
        scores = sc[b, 0, :, upto], sc[b, 1, :, upto]
        dq = mm3(weighted, cut(kk, upto), 1, 0) + mm3(cut(e, mine), result(0), 1, 1)
        g[0, mine] = (scale * dq).astype(BF16)
        dk = mm3(weighted, cut(q, mine), 0, 0)
        dv = mm3(scores, cut(e, mine), 0, 0)
        if b == 0:
            att[0, upto], att[1, upto] = dk, dv
            att[0, 256:], att[1, 256:] = jnp.zeros((2, 256, HD), F32)
            sum_two(2, later)
        else:
            att[0, upto] += dk
            att[1, upto] += dv
    send(g.at[0, core_rows(1 - k)], gx.at[0], sib_send.at[12], sib_recv.at[12], sibling)
    for at_n in range(3):
        arrived(w2.at[at_n], sib_recv.at[at_n])
    sum_three(2, later)
    suffix = result(2)

    def finish(kk, give_away):
        rows = core_rows(kk)
        for c, cols, turned in ((1, slice(HD, None), 1), (2, slice(HD), 0)):
            value = mm3(split(acc[0, rows, cols]), suffix, 1, turned)
            g[c, rows] = (scale * (att[c - 1, rows] + value)).astype(BF16)
            if give_away:
                send(g.at[c, rows], gx.at[c], sib_send.at[12 + c], sib_recv.at[12 + c], sibling)

    finish(1 - k, True)
    finish(k, False)
    arrived(gx.at[0], sib_recv.at[12])

    def beside(left, right):
        return jnp.concatenate([left, right], 1)

    def rows_of(ref, at_s, h):
        return ref[at_s, h // 2, pl.ds(2 * lax.rem(h, 2), 2)].reshape(512, HD)

    def own_term(by, start, size):
        h, few = zb(by), pl.ds(start, size)
        own = pl.ds(pl.multiple_of(256 * k + start, 128), size)
        return (
            mm(beside(g[1, own], g[2, own]), beside(rows_of(w, KP, h), rows_of(w, VP, h)), 1, 1)
            + mm(beside(g[0, own], gx[0, few]), beside(rows_of(w, QP, h), rows_of(w2, 2, h)), 1, 1)
        )

    def other_term(by, start, size):
        h, few = zb(by), pl.ds(start, size)
        return mm(beside(gx[1, few], gx[2, few]), beside(rows_of(w2, 0, h), rows_of(w2, 1, h)), 1, 1)

    def term(by, half):
        return own_term(by, 128 * half, 128) + other_term(by, 128 * half, 128)

    opposite = own_term(4, 0, 256)
    arrived(gx.at[1], sib_recv.at[13])
    arrived(gx.at[2], sib_recv.at[14])
    opposite = opposite + other_term(4, 0, 256)

    def hop(n, sign, out, inn, to, step, half):
        if step == 1:
            value = opposite[128 * half:128 * half + 128]
        else:
            value = term(sign * (5 - step), half)
        fresh = step == 1 or (step == 2 and half != n)
        if not fresh:
            arrived(inn.at[step - 2, half], rs_recv.at[n, step - 2, half])
            value = value + inn[step - 2, half].astype(F32)
        out[step - 1, half] = value.astype(BF16)
        send(
            out.at[step - 1, half], inn.at[step - 1, half],
            rs_send.at[n, step - 1, half], rs_recv.at[n, step - 1, half], to,
        )

    ways = ((0, 1, out_r, in_r, zr), (1, -1, out_l, in_l, zl))
    for step in range(1, 5):
        for turn_at in range(2):
            for n, sign, out, inn, to in ways:
                half = (1 - n) if turn_at == 0 else n
                if step == 1 and half != n:
                    continue
                hop(n, sign, out, inn, to, step, half)
    grad_ref[...] = own_term(0, 0, 256) + other_term(0, 0, 256)
    for turn_at in range(2):
        for n, _, _, inn, _ in ways:
            half = (1 - n) if turn_at == 0 else n
            few = slice(128 * half, 128 * half + 128)
            arrived(inn.at[3, half], rs_recv.at[n, 3, half])
            grad_ref[few] += inn[3, half].astype(F32)
    arrived(dgot, sib_recv.at[11])
    diff_ref[:, lanes(1 - k)] = dgot[...]
    for copy in sent:
        copy.wait_send()


def per_device(tokens, policy_weight, reference_weight):
    seq = tokens.shape[0] * lax.axis_size("ctx")
    scale = 1.0 / math.sqrt(HD * seq)

    whole = pltpu.VMEM((HD, HD), F32)
    some = lambda *lead: pltpu.VMEM((*lead, HD // 2, HD), F32)
    sums = (whole, some(2, 4), some(3), some(2, 4), whole)
    half = pltpu.VMEM((4, 2, 128, 512), BF16)
    dma = pltpu.SemaphoreType.DMA
    return pl.pallas_call(
        functools.partial(kernel, scale),
        out_shape=(
            pltpu.VMEM((256, 256), F32),
            pltpu.VMEM((256, 512), F32),
        ),
        in_specs=[pl.BlockSpec(memory_space=pl.ANY)] * 3,
        out_specs=[pl.BlockSpec(memory_space=pltpu.VMEM)] * 2,
        scratch_shapes=[
            pltpu.VMEM((6, 4, 4, 256, HD), BF16),
            pltpu.VMEM((3, 4, 4, 256, HD), BF16),
            pltpu.VMEM((6, 128, HD), BF16),
            pltpu.VMEM((16, 512, 256), BF16),
            pltpu.VMEM((3, 512, 2 * HD), F32),
            pltpu.VMEM((2, 512, HD), F32),
            pltpu.VMEM((2, 2, 256, 512), BF16),
            pltpu.VMEM((512, HD), F32),
            pltpu.VMEM((256, HD), F32),
            pltpu.VMEM((3, 512, HD), BF16),
            pltpu.VMEM((3, 256, HD), BF16),
            (sums, sums, sums),
            half, half, half, half,
            dma((14,)), dma((6,)), dma((6,)), dma((6, 6)), dma((6, 6)), dma((6, 6)), dma((6, 6)),
            dma((15,)), dma((15,)), dma((2, 4, 2)), dma((2, 4, 2)), dma((3, 12)), dma((3, 12)),
            dma((2, 4, 2)), dma((2, 4, 2)),
        ],
        compiler_params=pltpu.CompilerParams(
            collective_id=0, has_side_effects=True, vmem_limit_bytes=58 * 2**20
        ),
    )(tokens, policy_weight, reference_weight)


def solution(mesh):
    in_specs = (P("ctx", "head"), P(None, "ctx", "head"), P(None, "ctx", "head"))
    out_specs = (P("ctx", "head"), P("ctx", "head"))
    return jax.shard_map(
        per_device, mesh=mesh, in_specs=in_specs, out_specs=out_specs, check_vma=False
    )
```
